32 devices in a mesh: scen: 8 (over z, core), inst: 4 (over y, x).
Axes of the slice: x: 2, y: 2, z: 4, core: 2. Of those that a mesh axis runs over, the one named last changes fastest.
Arguments:
- shocks: bfloat16 [4096, 2048], P('scen', 'inst'), may hold values from -6 to 6
- loadings: bfloat16 [2048, 16384], P(None, 'inst'), may hold values from -0.125 to 0.125
- delta: float32 [16384], P('inst'), may hold values from -6 to 6
- gamma: float32 [16384], P('inst'), may hold values from -3 to 3
- kappa: float32 [16384], P('inst'), may hold values from -1.2 to 1.2
- book_of: int32 [16384], P('inst'), may hold values from 0 to 255
- bracket_low: int32 [256], replicated, may hold values from -48 to -25
- bracket_high: int32 [256], replicated, may hold values from -24 to 8
- rank: int32 [256], replicated, may hold values from 32 to 64
Outputs:
- contribution: float32 [256, 16384], P('scen', 'inst')
- quantile: float32 [256], P('inst')
The draws below stay inside these ranges and needn't reach their ends.
Inputs may be any that keep to these rules, and one draw needn't show every extreme that they name: `book_of`: each instrument's book.
All inputs are finite; a program needn't handle non-finite values.
Results may differ from the reference program's by a relative error of at most 0.002.
Values may be sent and summed in bfloat16 or wider, within the bound.
No kernel may reach another device: no remote copies, remote signals or barrier semaphores. Data moves between devices by JAX's collectives and lax.ppermute only.
A program may use at most 128 MiB of HBM per device.

```python
import jax
import jax.numpy as jnp
from jax import lax

FACTORS = 2048
BOOKS = 256
PIVOTS = 64
ROUNDS = 3
INST_DEV = 4096
SCEN = 4096
INST = 16384
N_INST = 4


def set_ends(array, own_key, smallest, high):
    longest = array.shape.index(max(array.shape))
    spots = []
    for shift in (0, 1):
        where = [jax.random.randint(jax.random.fold_in(own_key, axis), (), 0, length) for axis, length in enumerate(array.shape)]
        where[longest] = (where[longest] + shift) % array.shape[longest]
        spots.append(tuple(where))
    return array.at[spots[0]].set(smallest).at[spots[1]].set(high)


def block_levels(key, extent, shards, low, top_value):
    level, own = 1.0, jax.random.fold_in(key, 6)
    for axis_at, parts in shards:
        heights = jnp.exp(jax.random.uniform(jax.random.fold_in(own, axis_at), (parts,), jnp.float32, low / len(shards), top_value / len(shards)))
        level = level * jnp.repeat(heights, extent[axis_at] // parts).reshape([-1 if axis == axis_at else 1 for axis in range(len(extent))])
    return level


def noise(own_key, dims, scale, bound, split=(), held_as=jnp.bfloat16):
    factor_of = block_levels(own_key, dims, split, -0.22, 0.18) if split else 1.0
    array = jax.random.normal(own_key, dims, jnp.float32) * scale * factor_of
    return jnp.minimum(jnp.maximum(array, -bound), bound).astype(held_as)


def setup_inputs(seed: int = 0) -> dict:
    seeds = jax.random.split(jax.random.key(seed), 10)
    return {
        "shocks": noise(seeds[0], (SCEN, FACTORS), 1.0, 6.0, ((0, 8), (1, 4))),
        "loadings": noise(seeds[1], (FACTORS, INST), FACTORS ** -0.5, 0.125, ((1, 4),)),
        "delta": noise(seeds[2], (INST,), 1.0, 6.0, ((0, 4),), jnp.float32),
        "gamma": noise(seeds[3], (INST,), 0.5, 3.0, ((0, 4),), jnp.float32),
        "kappa": noise(seeds[4], (INST,), 0.2, 1.2, ((0, 4),), jnp.float32),
        "book_of": set_ends(jax.random.randint(seeds[5], (INST,), 0, BOOKS), jax.random.fold_in(seeds[5], 1), 0, BOOKS - 1).astype(jnp.int32),
        "bracket_low": set_ends(jax.random.randint(seeds[6], (BOOKS,), -48, -24), jax.random.fold_in(seeds[6], 1), -48, (-24) - 1).astype(jnp.int32),
        "bracket_high": set_ends(jax.random.randint(seeds[7], (BOOKS,), -24, 9), jax.random.fold_in(seeds[7], 1), -24, 8).astype(jnp.int32),
        "rank": set_ends(jax.random.randint(seeds[8], (BOOKS,), SCEN // 128, SCEN // 64 + 1), jax.random.fold_in(seeds[8], 1), SCEN // 128, (SCEN // 64 + 1) - 1).astype(jnp.int32),
    }


tail_width = 0.5
bracket_unit = 0.125


def revalue(moves, delta, gamma, kappa):
    return (moves * (delta + moves * (gamma + moves * kappa))).astype(jnp.bfloat16)


def count_below(book_pnl, pivots):
    group = min(book_pnl.shape[1], 32)
    blocks = book_pnl.T.reshape(-1, group, book_pnl.shape[0])
    pivot_blocks = pivots.reshape(-1, group, pivots.shape[1])

    def one_block(pair):
        values, marks = pair
        return jnp.sum((values[:, :, None] <= marks[:, None, :]).astype(jnp.int32), axis=1)

    return lax.map(one_block, (blocks, pivot_blocks)).reshape(pivots.shape)


def locate(book_pnl, bracket_low, bracket_high, rank, total):
    lower = bracket_low.astype(jnp.float32) * bracket_unit
    upper = bracket_high.astype(jnp.float32) * bracket_unit
    marks = jnp.arange(PIVOTS, dtype=jnp.int32)
    levels = marks.astype(jnp.float32)
    for sweep_index in range(ROUNDS):
        spacing = (upper - lower) / (PIVOTS - 1)
        pivots = lower[:, None] + levels[None, :] * spacing[:, None]
        counts = total(count_below(book_pnl, pivots))
        below = jnp.sum((counts < rank[:, None]).astype(jnp.int32), axis=1)
        chosen = jnp.clip(below, 1, PIVOTS - 1)
        lower = jnp.sum(jnp.where(marks[None, :] == (chosen - 1)[:, None], pivots, 0.0), axis=1)
        upper = jnp.sum(jnp.where(marks[None, :] == chosen[:, None], pivots, 0.0), axis=1)
    return (lower + upper) * 0.5


def reference(shocks, loadings, delta, gamma, kappa, book_of, bracket_low, bracket_high, rank):
    width = INST_DEV
    blocks = N_INST
    scale = (BOOKS / (width * blocks)) ** 0.5
    load_blocks = loadings.reshape(FACTORS, blocks, width).transpose(1, 0, 2)
    books = jnp.arange(BOOKS, dtype=jnp.int32)

    def one_block(pieces):
        load_part, delta_part, gamma_part, kappa_part, book_part = pieces
        moves = jnp.dot(shocks, load_part, preferred_element_type=jnp.float32)
        profit = revalue(moves, delta_part, gamma_part, kappa_part)
        onehot = (book_part[:, None] == books[None, :]).astype(jnp.bfloat16)
        return profit, jnp.dot(profit, onehot, preferred_element_type=jnp.float32) * scale

    profit_blocks, partials = lax.map(one_block, (load_blocks, delta.reshape(blocks, width), gamma.reshape(blocks, width), kappa.reshape(blocks, width), book_of.reshape(blocks, width)))
    book_pnl = jnp.sum(partials, axis=0)
    quantile = locate(book_pnl, bracket_low, bracket_high, rank, lambda counts: counts)
    weights = jax.nn.sigmoid((quantile[None, :] - book_pnl) / tail_width).astype(jnp.bfloat16)
    mass = jnp.sum(weights.astype(jnp.float32), axis=0)

    def tail_block(profit):
        return lax.dot_general(weights, profit, (((0,), (0,)), ((), ())), preferred_element_type=jnp.float32)

    terms = lax.map(tail_block, profit_blocks)
    contribution = terms.transpose(1, 0, 2).reshape(BOOKS, blocks * width) / mass[:, None]
    return contribution, quantile
```

```python
import functools

import jax
import jax.numpy as jnp
from jax import lax
from jax.experimental import pallas as pl
from jax.experimental.pallas import tpu as pltpu
from jax.sharding import PartitionSpec as P

PIVOTS = 64
ROUNDS = 3
CORES = 2
LANES = 128

tail_width = 0.5
bracket_unit = 0.125
code_top = 65535.0
code_mid = 32768.0
top16 = 32600.0
octave = 0.6931471805599453
finest = 8.0
half_word = 16384.0

BF16 = jnp.bfloat16
F32 = jnp.float32


def params(megabytes):
    return pltpu.CompilerParams(vmem_limit_bytes=megabytes * 2**20)


def dot(a, b):
    return jnp.dot(a, b, preferred_element_type=F32)


def dot_nt(a, b):
    return lax.dot_general(a, b, (((1,), (1,)), ((), ())), preferred_element_type=F32)


def swap(value, axis, flip):
    n = lax.axis_size(axis)
    return lax.ppermute(value, axis, [(k, k ^ flip) for k in range(n)])


def first_moves_kernel(count, where_ref, *refs):
    shock_refs, load_refs, out_ref = refs[:count], refs[count : 2 * count], refs[2 * count]
    total = dot(shock_refs[0][...], load_refs[0][...])
    for shock_ref, load_ref in zip(shock_refs[1:], load_refs[1:]):
        total = total + dot(shock_ref[...], load_ref[...])
    out_ref[...] = total


def first_moves(where, shocks, flips, loadings, tile):
    rows, depth = shocks[0].shape
    cols = loadings.shape[1]
    count = len(shocks)
    steps = cols // tile
    col_of = functools.partial(column_tile, steps)
    specs = [pl.BlockSpec((rows, depth), lambda n, w: (0, 0)) for _ in shocks]
    specs += [
        pl.BlockSpec((depth, tile), lambda n, w, f=f: (w[0] ^ f, col_of(n, w))) for f in flips
    ]
    return pl.pallas_call(
        functools.partial(first_moves_kernel, count),
        out_shape=jax.ShapeDtypeStruct((rows, cols), F32),
        grid_spec=pltpu.PrefetchScalarGridSpec(
            num_scalar_prefetch=1,
            grid=(steps,),
            in_specs=specs,
            out_specs=pl.BlockSpec((rows, tile), lambda n, w: (0, n)),
        ),
        compiler_params=params(48),
        cost_estimate=pl.CostEstimate(
            flops=2 * rows * depth * cols * count,
            bytes_accessed=2 * depth * cols * count + 4 * rows * cols,
            transcendentals=0,
        ),
        name="first_moves",
    )(where, *shocks, *([loadings] * count))


def column_tile(steps, n, where_ref):
    return lax.rem(n + (1 - where_ref[1]) * (steps // CORES), steps)


def profit_kernel(count, slots, where_ref, *refs):
    top_refs, low_refs, load_refs = refs[:count], refs[count : 2 * count], refs[2 * count : 3 * count]
    first_ref, delta_ref, gamma_ref, kappa_ref, book_ref = refs[3 * count : 3 * count + 5]
    mine_ref, theirs_ref = refs[3 * count + 5 : 3 * count + 7]
    sum_refs = refs[3 * count + 7 :]
    step = pl.program_id(0)
    share = sum_refs[0].shape[0]
    half = top_refs[0].shape[0]
    tile = first_ref.shape[1]

    @pl.when(step == 0)
    def _():
        for sum_ref in sum_refs:
            sum_ref[...] = jnp.zeros_like(sum_ref)

    parts = []
    for at, shock_refs in ((0, top_refs), (half, low_refs)):
        moves = first_ref[at : at + half, :]
        for shock_ref, load_ref in zip(shock_refs, load_refs):
            moves = moves + dot(shock_ref[...], load_ref[...])
        value = moves * (delta_ref[...] + moves * (gamma_ref[...] + moves * kappa_ref[...]))
        parts.append(value.astype(BF16))
    profit = jnp.concatenate(parts, axis=0)

    @pl.when(step < pl.num_programs(0) // CORES)
    def _():
        theirs_ref[...] = profit

    @pl.when(step >= pl.num_programs(0) // CORES)
    def _():
        mine_ref[...] = profit

    row = lax.broadcasted_iota(jnp.int32, (share, tile), 0)
    for slot in range(slots):
        start = (where_ref[0] ^ slot) * share
        onehot = jnp.where(row + start == book_ref[...], 1.0, 0.0).astype(BF16)
        sum_refs[slot][...] += dot_nt(onehot, profit)


def profits(where, tops, lows, flips, loadings, first, delta, gamma, kappa, book_of, slots, books, tile):
    half, depth = tops[0].shape
    rows, cols = first.shape
    count = len(tops)
    steps = cols // tile
    col_of = functools.partial(column_tile, steps)
    share = books // slots
    line = pl.BlockSpec((1, tile), lambda n, w: (0, col_of(n, w)))
    specs = [pl.BlockSpec((half, depth), lambda n, w: (0, 0)) for _ in range(2 * count)]
    specs += [
        pl.BlockSpec((depth, tile), lambda n, w, f=f: (w[0] ^ f, col_of(n, w))) for f in flips
    ]
    specs += [pl.BlockSpec((rows, tile), lambda n, w: (0, n)), line, line, line, line]
    part = steps // CORES
    out_specs = [
        pl.BlockSpec((rows, tile), lambda n, w: (0, jnp.maximum(n - part, 0))),
        pl.BlockSpec((rows, tile), lambda n, w: (0, jnp.minimum(n, part - 1))),
    ]
    out_specs += [pl.BlockSpec((share, rows), lambda n, w: (0, 0)) for _ in range(slots)]
    out_shape = [jax.ShapeDtypeStruct((rows, cols // CORES), BF16)] * 2
    out_shape += [jax.ShapeDtypeStruct((share, rows), F32)] * slots
    return pl.pallas_call(
        functools.partial(profit_kernel, count, slots),
        out_shape=out_shape,
        grid_spec=pltpu.PrefetchScalarGridSpec(
            num_scalar_prefetch=1, grid=(steps,), in_specs=specs, out_specs=out_specs
        ),
        compiler_params=params(48),
        cost_estimate=pl.CostEstimate(
            flops=2 * rows * cols * (depth * count + books),
            bytes_accessed=2 * depth * cols * count + 6 * rows * cols,
            transcendentals=0,
        ),
        name="profits",
    )(where, *tops, *lows, *([loadings] * count), first, delta, gamma, kappa, book_of)


def gather_and_revalue(where, shocks, loadings, delta, gamma, kappa, book_of, books):
    slots = lax.axis_size("inst")
    inner = 1
    while inner * inner * 4 <= slots:
        inner *= 2
    outer = slots // inner
    rows = shocks.shape[0]
    half = rows // 2
    along = [f for f in range(1, inner)]
    across = [f * inner for f in range(1, outer)]
    near = {f: swap(shocks, "inst", f) for f in along + across}
    corners = [(a, b) for a in along for b in across]
    tops = [swap(near[a][:half], "inst", b) for a, b in corners]
    lows = [swap(near[b][half:], "inst", a) for a, b in corners]
    flips = [0] + along + across
    first = first_moves(where, [shocks] + [near[f] for f in along + across], flips, loadings, 512)
    return profits(
        where, tops, lows, [a ^ b for a, b in corners], loadings, first, delta, gamma, kappa, book_of, slots, books, 512
    )


def book_value_kernel(scale, low_ref, high_ref, *refs):
    part_refs, (value_ref, code_ref) = refs[:-2], refs[-2:]
    value = part_refs[0][...]
    for part_ref in part_refs[1:]:
        value = value + part_ref[...]
    value = value * scale
    value_ref[...] = value
    low = low_ref[...].astype(F32) * bracket_unit
    high = high_ref[...].astype(F32) * bracket_unit
    code = (value - low) * (code_top / (high - low))
    code = jnp.minimum(jnp.maximum(code, 0.0), code_top)
    code_ref[...] = (jnp.round(code) - code_mid).astype(jnp.int32).astype(jnp.int16)


def book_values(scale, low, high, parts):
    share, rows = parts[0].shape
    return pl.pallas_call(
        functools.partial(book_value_kernel, scale),
        out_shape=[
            jax.ShapeDtypeStruct((share, rows), F32),
            jax.ShapeDtypeStruct((share, rows), jnp.int16),
        ],
        compiler_params=params(16),
        name="book_values",
    )(low, high, *parts)


def quantile_kernel(low_ref, high_ref, rank_ref, value_ref, *refs):
    code_refs, (weight_ref, quantile_ref, held) = refs[:-3], refs[-3:]
    share, rows = value_ref.shape
    for at, code_ref in enumerate(code_refs):
        held[:, at * rows : (at + 1) * rows] = code_ref[...].astype(F32)
    width = held.shape[1]
    low = low_ref[...].astype(F32) * bracket_unit
    high = high_ref[...].astype(F32) * bracket_unit
    rank = rank_ref[...].astype(F32)
    per_unit = code_top / (high - low)
    lower, upper = low, high
    for _ in range(ROUNDS):
        spacing = (upper - lower) / (PIVOTS - 1)
        below = jnp.zeros_like(low)
        stride = PIVOTS // 2
        while stride:
            pivot = lower + (below + (stride - 1)) * spacing
            mark = jnp.floor((pivot - low) * per_unit) - code_mid
            mark = jnp.broadcast_to(mark, (share, LANES))
            count = jnp.zeros((share, LANES), F32)
            for at in range(0, width, LANES):
                count = count + jnp.where(held[:, at : at + LANES] <= mark, 1.0, 0.0)
            count = jnp.sum(count, axis=1, keepdims=True)
            below = below + jnp.where(count < rank, float(stride), 0.0)
            stride //= 2
        chosen = jnp.clip(below, 1.0, float(PIVOTS - 1))
        lower, upper = lower + (chosen - 1.0) * spacing, lower + chosen * spacing
    quantile = (lower + upper) * 0.5
    quantile_ref[...] = quantile
    weight_ref[...] = jax.nn.sigmoid((quantile - value_ref[...]) / tail_width).astype(BF16)


def quantiles(low, high, rank, value, codes):
    share, rows = value.shape
    return pl.pallas_call(
        quantile_kernel,
        out_shape=[
            jax.ShapeDtypeStruct((share, rows), BF16),
            jax.ShapeDtypeStruct((share, 1), F32),
        ],
        scratch_shapes=[pltpu.VMEM((share, rows * len(codes)), F32)],
        compiler_params=params(16),
        name="quantiles",
    )(low, high, rank, value, *codes)


def encode(total, mass):
    top = jnp.maximum(jnp.max(jnp.abs(total), axis=1, keepdims=True), 1e-30)
    level = jnp.ceil(jnp.log(top * (1.0 / top16)) * (finest / octave))
    words = jnp.round(total * jnp.exp(level * (-octave / finest)))
    mass = jnp.maximum(mass, 1e-30)
    power = jnp.ceil(jnp.log(mass) * (1.0 / octave))
    scaled = mass * jnp.exp(power * -octave) * half_word
    upper = jnp.floor(scaled)
    lower = jnp.round((scaled - upper) * half_word)
    column = lax.broadcasted_iota(jnp.int32, (total.shape[0], LANES), 1)
    side = jnp.where(column == 0, level, 0.0)
    side = jnp.where(column == 1, power, side)
    side = jnp.where(column == 2, upper, side)
    side = jnp.where(column == 3, lower, side)
    return words.astype(jnp.int32).astype(jnp.int16), side.astype(jnp.int32).astype(jnp.int16)


def put_words(ref, total, mass):
    words, side = encode(total, mass)
    cols = total.shape[1]
    ref[:, :cols] = words
    ref[:, cols:] = side


def get_words(ref):
    cols = ref.shape[1] - LANES
    side = ref[:, cols:].astype(F32)
    level, power, upper, lower = (side[:, k : k + 1] for k in range(4))
    mass = (upper + lower * (1.0 / half_word)) * (1.0 / half_word) * jnp.exp(power * octave)
    total = ref[:, :cols].astype(F32) * jnp.exp(level * (octave / finest))
    return total, mass


def put_plain(ref, total, mass):
    cols = total.shape[1]
    ref[:, :cols] = total
    ref[:, cols:] = jnp.broadcast_to(mass, (total.shape[0], LANES))


def get_plain(ref):
    cols = ref.shape[1] - LANES
    return ref[:, :cols], ref[:, cols : cols + 1]


def tail_kernel(slots, lines, where_ref, *refs):
    count = CORES * slots
    weight_refs = refs[:count]
    profit_refs = refs[count : count + CORES]
    away_ref, partner_ref, handled_ref, own_ref, held, total = refs[count + CORES :]
    step = pl.program_id(0)
    share, rows = weight_refs[0].shape
    books = share * slots
    block = books // lines
    piece = min(share, block)
    tile = profit_refs[0].shape[1]

    @pl.when(step == 0)
    def _():
        for core in range(CORES):
            for slot in range(slots):
                ref = weight_refs[core * slots + slot]
                for at in range(0, share, piece):
                    start = (where_ref[0] ^ slot) * share + at
                    line = start // block
                    to = (where_ref[2] ^ line) * block + (start - line * block)
                    to = pl.multiple_of(to, piece)
                    held[pl.ds(to, piece), core * rows : (core + 1) * rows] = ref[at : at + piece, :]

    spot = pl.multiple_of(step * tile, tile)
    result = dot(held[:, :rows], profit_refs[0][...])
    total[:, pl.ds(spot, tile)] = result + dot(held[:, rows:], profit_refs[1][...])

    @pl.when(step == pl.num_programs(0) - 1)
    def _():
        for line in range(lines):
            at = line * block
            value = total[at : at + block, :]
            mass = jnp.sum(held[at : at + block, :].astype(F32), axis=1, keepdims=True)
            to = (line // 2 - 1) * block
            if line == 0:
                put_plain(own_ref, value, mass)
            elif line == 1:
                put_words(partner_ref, value, mass)
            elif line % 2 == 0:
                put_words(away_ref.at[to : to + block], value, mass)
            else:
                put_plain(handled_ref.at[to : to + block], value, mass)


def tail_sums(where, weights, profit_pair, slots, lines, tile):
    share, rows = weights[0].shape
    cols = profit_pair[0].shape[1]
    books = share * slots
    block = books // lines
    others = lines // 2 - 1
    wide = cols + LANES
    specs = [pl.BlockSpec((share, rows), lambda n, w: (0, 0)) for _ in weights]
    specs += [pl.BlockSpec((rows, tile), lambda n, w: (0, n)) for _ in profit_pair]
    shapes = [
        ((others * block, wide), jnp.int16),
        ((block, wide), jnp.int16),
        ((others * block, wide), F32),
        ((block, wide), F32),
    ]
    return pl.pallas_call(
        functools.partial(tail_kernel, slots, lines),
        out_shape=[jax.ShapeDtypeStruct(*shape) for shape in shapes],
        grid_spec=pltpu.PrefetchScalarGridSpec(
            num_scalar_prefetch=1,
            grid=(cols // tile,),
            in_specs=specs,
            out_specs=[pl.BlockSpec(shape, lambda n, w: (0, 0)) for shape, _ in shapes],
            scratch_shapes=[
                pltpu.VMEM((books, CORES * rows), BF16),
                pltpu.VMEM((books, cols), F32),
            ],
        ),
        compiler_params=params(48),
        name="tail_sums",
    )(where, *weights, *profit_pair)


def relay_kernel(words_ref, plain_ref, out_ref):
    total, mass = get_words(words_ref)
    own_total, own_mass = get_plain(plain_ref)
    put_words(out_ref, total + own_total, mass + own_mass)


def relay(words, plain):
    return pl.pallas_call(
        relay_kernel,
        out_shape=jax.ShapeDtypeStruct(words.shape, jnp.int16),
        compiler_params=params(16),
        name="relay",
    )(words, plain)


def finish_kernel(where_ref, plain_ref, *refs):
    words_refs, (keep_ref, give_ref, held) = refs[:-3], refs[-3:]
    total, mass = get_plain(plain_ref)
    for words_ref in words_refs:
        more, more_mass = get_words(words_ref)
        total, mass = total + more, mass + more_mass
    held[...] = total / mass
    rows = keep_ref.shape[0]
    keep_ref[...] = held[pl.ds(pl.multiple_of(where_ref[1] * rows, rows), rows), :]
    give_ref[...] = held[pl.ds(pl.multiple_of((1 - where_ref[1]) * rows, rows), rows), :]


def finish(where, plain, words):
    block, wide = plain.shape
    cols = wide - LANES
    vmem = pl.BlockSpec(memory_space=pltpu.VMEM)
    return pl.pallas_call(
        finish_kernel,
        out_shape=[jax.ShapeDtypeStruct((block // CORES, cols), F32)] * 2,
        in_specs=[pl.BlockSpec(memory_space=pltpu.SMEM)] + [vmem] * (1 + len(words)),
        out_specs=[vmem] * 2,
        scratch_shapes=[pltpu.VMEM((block, cols), F32)],
        compiler_params=params(16),
        name="finish",
    )(where, plain, *words)


def body(shocks, loadings, delta, gamma, kappa, book_of, bracket_low, bracket_high, rank):
    inst_cols = loadings.shape[1]
    books = bracket_low.shape[0]
    slots = lax.axis_size("inst")
    lines = lax.axis_size("scen") // CORES
    share = books // slots
    scale = (books / (inst_cols * slots)) ** 0.5
    inst = lax.axis_index("inst")
    scen = lax.axis_index("scen")
    core, line = scen % CORES, scen // CORES
    where = jnp.stack([inst, core, line]).astype(jnp.int32)

    mine, theirs, *sums = gather_and_revalue(
        where,
        shocks,
        loadings,
        delta[None, :],
        gamma[None, :],
        kappa[None, :],
        book_of[None, :],
        books,
    )
    got = swap(theirs, "scen", 1)

    own = lambda v: lax.dynamic_slice_in_dim(v, inst * share, share, 0)[:, None]
    low, high, own_rank = own(bracket_low), own(bracket_high), own(rank)
    parts = [sums[0]] + [swap(sums[slot], "inst", slot) for slot in range(1, slots)]
    value, code = book_values(scale, low, high, parts)
    codes = [code] + [swap(code, "scen", CORES * k) for k in range(1, lines)]
    codes = codes + [swap(c, "scen", 1) for c in codes]
    weight, quantile = quantiles(low, high, own_rank, value, codes)
    weights = [weight] + [swap(weight, "inst", slot) for slot in range(1, slots)]
    others = [swap(w, "scen", 1) for w in weights]

    away, partner, handled, plain = tail_sums(where, weights + others, [mine, got], slots, lines, 512)
    passed = swap(away, "scen", CORES)
    from_partner = swap(partner, "scen", CORES)
    sent = relay(passed, handled)
    block = books // lines
    words = [from_partner]
    for k in range(1, lines // 2):
        words.append(swap(sent[(k - 1) * block : k * block], "scen", CORES * (2 * k + 1)))
    keep, give = finish(where, plain, words)
    taken = swap(give, "scen", 1)
    left = jnp.where(core == 0, keep, taken)
    right = jnp.where(core == 0, taken, keep)
    return jnp.concatenate([left, right], axis=1), quantile[:, 0]


def solution(mesh):
    placed = (
        P("scen", "inst"),
        P(None, "inst"),
        P("inst"),
        P("inst"),
        P("inst"),
        P("inst"),
        P(),
        P(),
        P(),
    )
    return jax.shard_map(
        body, mesh=mesh, in_specs=placed, out_specs=(P("scen", "inst"), P("inst")), check_vma=False
    )
```

```python
import functools

import jax
import jax.numpy as jnp
from jax import lax
from jax.experimental import pallas as pl
from jax.experimental.pallas import tpu as pltpu
from jax.sharding import PartitionSpec as P

PIVOTS = 64
ROUNDS = 3
CORES = 2
LANES = 128

tail_width = 0.5
bracket_unit = 0.125
code_top = 65535.0
code_mid = 32768.0
top16 = 32600.0
octave = 0.6931471805599453
finest = 8.0
half_word = 16384.0

BF16 = jnp.bfloat16
F32 = jnp.float32


def params(megabytes):
    return pltpu.CompilerParams(vmem_limit_bytes=megabytes * 2**20)


def dot(a, b):
    return jnp.dot(a, b, preferred_element_type=F32)


def dot_nt(a, b):
    return lax.dot_general(a, b, (((1,), (1,)), ((), ())), preferred_element_type=F32)


def swap(value, axis, flip):
    n = lax.axis_size(axis)
    return lax.ppermute(value, axis, [(k, k ^ flip) for k in range(n)])


def tiles(width, tile):
    return [slice(at, at + tile) for at in range(0, width, tile)]


def stage_kernel(slots, near, far, where_ref, shocks_ref, book_ref, loadings_ref, first_ref, near_ref, far_ref, onehot_ref, own, sems):
    depth = shocks_ref.shape[1]
    books, cols = onehot_ref.shape
    share = books // slots
    rows_of = lambda flip: pl.ds(pl.multiple_of((where_ref[0] ^ flip) * depth, depth), depth)
    parts = tiles(cols, cols // 4)
    own_copies = [
        pltpu.make_async_copy(loadings_ref.at[rows_of(0), part], own.at[:, part], sems.at[k])
        for k, part in enumerate(parts)
    ]
    rest_copies = [
        pltpu.make_async_copy(
            loadings_ref.at[rows_of(flip), :],
            ref.at[k * depth : (k + 1) * depth, :],
            sems.at[len(parts) + flip - 1],
        )
        for ref, flips in ((near_ref, near), (far_ref, far))
        for k, flip in enumerate(flips)
    ]
    for copy in own_copies + rest_copies:
        copy.start()
    tile = cols // 8
    row = lax.broadcasted_iota(jnp.int32, (books, tile), 0)
    row = ((row // share) ^ where_ref[0]) * share + row % share
    for part in tiles(cols, tile):
        onehot_ref[:, part] = jnp.where(row == book_ref[:, part], 1.0, 0.0).astype(BF16)
    for copy, part in zip(own_copies, parts):
        copy.wait()
        first_ref[:, part] = dot(shocks_ref[...], own[:, part])
    for copy in rest_copies:
        copy.wait()


def stage(where, shocks, book_of, loadings, slots, near, far, books):
    rows, depth = shocks.shape
    cols = loadings.shape[1]
    vmem = pl.BlockSpec(memory_space=pltpu.VMEM)
    return pl.pallas_call(
        functools.partial(stage_kernel, slots, near, far),
        out_shape=[
            jax.ShapeDtypeStruct((rows, cols), F32),
            jax.ShapeDtypeStruct((len(near) * depth, cols), BF16),
            jax.ShapeDtypeStruct((len(far) * depth, cols), BF16),
            jax.ShapeDtypeStruct((books, cols), BF16),
        ],
        in_specs=[pl.BlockSpec(memory_space=pltpu.SMEM), vmem, vmem, pl.BlockSpec(memory_space=pltpu.HBM)],
        out_specs=[vmem] * 4,
        scratch_shapes=[pltpu.VMEM((depth, cols), BF16), pltpu.SemaphoreType.DMA((3 + slots,))],
        compiler_params=params(16),
        cost_estimate=pl.CostEstimate(
            flops=2 * rows * depth * cols, bytes_accessed=2 * loadings.size, transcendentals=0
        ),
        name="stage",
    )(where, shocks, book_of, loadings)


def add_moves_kernel(*refs):
    shock_refs, (rest_ref, before_ref, after_ref) = refs[:-3], refs[-3:]
    depth = shock_refs[0].shape[1]
    cols = after_ref.shape[1]
    for part in tiles(cols, cols // 8):
        total = before_ref[:, part]
        for k, shock_ref in enumerate(shock_refs):
            total = total + dot(shock_ref[...], rest_ref[k * depth : (k + 1) * depth, part])
        after_ref[:, part] = total


def add_moves(shocks, rest, before):
    vmem = pl.BlockSpec(memory_space=pltpu.VMEM)
    rows, cols = before.shape
    depth = shocks[0].shape[1]
    return pl.pallas_call(
        add_moves_kernel,
        out_shape=jax.ShapeDtypeStruct((rows, cols), F32),
        in_specs=[vmem] * (len(shocks) + 2),
        out_specs=vmem,
        input_output_aliases={len(shocks) + 1: 0},
        compiler_params=params(16),
        cost_estimate=pl.CostEstimate(
            flops=2 * rows * depth * cols * len(shocks), bytes_accessed=8 * rows * cols, transcendentals=0
        ),
        name="add_moves",
    )(*shocks, rest, before)


def profit_kernel(count, where_ref, *refs):
    top_refs, low_refs = refs[:count], refs[count : 2 * count]
    rest_ref, first_ref, delta_ref, gamma_ref, kappa_ref, onehot_ref = refs[2 * count : 2 * count + 6]
    mine_ref, theirs_ref = refs[2 * count + 6 : 2 * count + 8]
    sum_refs, total = refs[2 * count + 8 : -1], refs[-1]
    half, depth = top_refs[0].shape
    part_cols = mine_ref.shape[1]
    tile = part_cols // 4
    share = sum_refs[0].shape[0]
    fresh = True
    for side, out_ref in ((1 - where_ref[1], theirs_ref), (where_ref[1], mine_ref)):
        for spot in tiles(part_cols, tile):
            part = pl.ds(pl.multiple_of(side * part_cols + spot.start, tile), tile)
            pieces = []
            for at, shock_refs in ((0, top_refs), (half, low_refs)):
                moves = first_ref[at : at + half, part]
                for k, shock_ref in enumerate(shock_refs):
                    moves = moves + dot(shock_ref[...], rest_ref[k * depth : (k + 1) * depth, part])
                value = moves * (delta_ref[:, part] + moves * (gamma_ref[:, part] + moves * kappa_ref[:, part]))
                pieces.append(value.astype(BF16))
            profit = jnp.concatenate(pieces, axis=0)
            out_ref[:, spot] = profit
            sums = dot_nt(onehot_ref[:, part], profit)
            total[...] = sums if fresh else total[...] + sums
            fresh = False
    for slot, sum_ref in enumerate(sum_refs):
        sum_ref[...] = total[slot * share : (slot + 1) * share, :]


def profits(where, tops, lows, rest, first, delta, gamma, kappa, onehot, slots):
    rows, cols = first.shape
    books = onehot.shape[0]
    depth = tops[0].shape[1]
    vmem = pl.BlockSpec(memory_space=pltpu.VMEM)
    out_shape = [jax.ShapeDtypeStruct((rows, cols // CORES), BF16)] * 2
    out_shape += [jax.ShapeDtypeStruct((books // slots, rows), F32)] * slots
    return pl.pallas_call(
        functools.partial(profit_kernel, len(tops)),
        out_shape=out_shape,
        in_specs=[pl.BlockSpec(memory_space=pltpu.SMEM)] + [vmem] * (2 * len(tops) + 6),
        out_specs=[vmem] * len(out_shape),
        scratch_shapes=[pltpu.VMEM((books, rows), F32)],
        compiler_params=params(16),
        cost_estimate=pl.CostEstimate(
            flops=2 * rows * cols * (depth * len(tops) + books),
            bytes_accessed=6 * rows * cols,
            transcendentals=0,
        ),
        name="profits",
    )(where, *tops, *lows, rest, first, delta, gamma, kappa, onehot)


def gather_and_revalue(where, shocks, loadings, delta, gamma, kappa, book_of, books):
    slots = lax.axis_size("inst")
    inner = 1
    while inner * inner * 4 <= slots:
        inner *= 2
    outer = slots // inner
    half = shocks.shape[0] // 2
    along = [f for f in range(1, inner)]
    across = [f * inner for f in range(1, outer)]
    corners = [(a, b) for a in along for b in across]
    near = {f: swap(shocks, "inst", f) for f in along + across}
    first, near_loads, far_loads, onehot = stage(
        where, shocks, book_of, loadings, slots, along + across, [a ^ b for a, b in corners], books
    )
    tops = [swap(near[a][:half], "inst", b) for a, b in corners]
    lows = [swap(near[b][half:], "inst", a) for a, b in corners]
    first = add_moves([near[f] for f in along + across], near_loads, first)
    return profits(where, tops, lows, far_loads, first, delta, gamma, kappa, onehot, slots)


def book_value_kernel(scale, low_ref, high_ref, *refs):
    part_refs, (value_ref, code_ref) = refs[:-2], refs[-2:]
    value = part_refs[0][...]
    for part_ref in part_refs[1:]:
        value = value + part_ref[...]
    value = value * scale
    value_ref[...] = value
    low = low_ref[...].astype(F32) * bracket_unit
    high = high_ref[...].astype(F32) * bracket_unit
    code = (value - low) * (code_top / (high - low))
    code = jnp.minimum(jnp.maximum(code, 0.0), code_top)
    code_ref[...] = (jnp.round(code) - code_mid).astype(jnp.int32).astype(jnp.int16)


def book_values(scale, low, high, parts):
    share, rows = parts[0].shape
    return pl.pallas_call(
        functools.partial(book_value_kernel, scale),
        out_shape=[
            jax.ShapeDtypeStruct((share, rows), F32),
            jax.ShapeDtypeStruct((share, rows), jnp.int16),
        ],
        compiler_params=params(16),
        name="book_values",
    )(low, high, *parts)


def quantile_kernel(low_ref, high_ref, rank_ref, value_ref, *refs):
    code_refs, (weight_ref, quantile_ref, held) = refs[:-3], refs[-3:]
    share, rows = value_ref.shape
    for at, code_ref in enumerate(code_refs):
        held[:, at * rows : (at + 1) * rows] = code_ref[...].astype(F32)
    width = held.shape[1]
    low = low_ref[...].astype(F32) * bracket_unit
    high = high_ref[...].astype(F32) * bracket_unit
    rank = rank_ref[...].astype(F32)
    per_unit = code_top / (high - low)
    lower, upper = low, high
    for _ in range(ROUNDS):
        spacing = (upper - lower) / (PIVOTS - 1)
        below = jnp.zeros_like(low)
        stride = PIVOTS // 2
        while stride:
            pivot = lower + (below + (stride - 1)) * spacing
            mark = jnp.floor((pivot - low) * per_unit) - code_mid
            mark = jnp.broadcast_to(mark, (share, LANES))
            count = jnp.zeros((share, LANES), F32)
            for at in range(0, width, LANES):
                count = count + jnp.where(held[:, at : at + LANES] <= mark, 1.0, 0.0)
            count = jnp.sum(count, axis=1, keepdims=True)
            below = below + jnp.where(count < rank, float(stride), 0.0)
            stride //= 2
        chosen = jnp.clip(below, 1.0, float(PIVOTS - 1))
        lower, upper = lower + (chosen - 1.0) * spacing, lower + chosen * spacing
    quantile = (lower + upper) * 0.5
    quantile_ref[...] = quantile
    weight_ref[...] = jax.nn.sigmoid((quantile - value_ref[...]) / tail_width).astype(BF16)


def quantiles(low, high, rank, value, codes):
    share, rows = value.shape
    return pl.pallas_call(
        quantile_kernel,
        out_shape=[
            jax.ShapeDtypeStruct((share, rows), BF16),
            jax.ShapeDtypeStruct((share, 1), F32),
        ],
        scratch_shapes=[pltpu.VMEM((share, rows * len(codes)), F32)],
        compiler_params=params(16),
        name="quantiles",
    )(low, high, rank, value, *codes)


def encode(total, mass):
    top = jnp.maximum(jnp.max(jnp.abs(total), axis=1, keepdims=True), 1e-30)
    level = jnp.ceil(jnp.log(top * (1.0 / top16)) * (finest / octave))
    words = jnp.round(total * jnp.exp(level * (-octave / finest)))
    mass = jnp.maximum(mass, 1e-30)
    power = jnp.ceil(jnp.log(mass) * (1.0 / octave))
    scaled = mass * jnp.exp(power * -octave) * half_word
    upper = jnp.floor(scaled)
    lower = jnp.round((scaled - upper) * half_word)
    column = lax.broadcasted_iota(jnp.int32, (total.shape[0], LANES), 1)
    side = jnp.where(column == 0, level, 0.0)
    side = jnp.where(column == 1, power, side)
    side = jnp.where(column == 2, upper, side)
    side = jnp.where(column == 3, lower, side)
    return words.astype(jnp.int32).astype(jnp.int16), side.astype(jnp.int32).astype(jnp.int16)


def put_words(ref, total, mass):
    words, side = encode(total, mass)
    cols = total.shape[1]
    ref[:, :cols] = words
    ref[:, cols:] = side


def get_words(ref):
    cols = ref.shape[1] - LANES
    side = ref[:, cols:].astype(F32)
    level, power, upper, lower = (side[:, k : k + 1] for k in range(4))
    mass = (upper + lower * (1.0 / half_word)) * (1.0 / half_word) * jnp.exp(power * octave)
    total = ref[:, :cols].astype(F32) * jnp.exp(level * (octave / finest))
    return total, mass


def put_plain(ref, total, mass):
    cols = total.shape[1]
    ref[:, :cols] = total
    ref[:, cols:] = jnp.broadcast_to(mass, (total.shape[0], LANES))


def get_plain(ref):
    cols = ref.shape[1] - LANES
    return ref[:, :cols], ref[:, cols : cols + 1]


def tail_kernel(slots, lines, where_ref, *refs):
    count = CORES * slots
    weight_refs = refs[:count]
    profit_refs = refs[count : count + CORES]
    away_ref, partner_ref, handled_ref, own_ref, held, total = refs[count + CORES :]
    step = pl.program_id(0)
    share, rows = weight_refs[0].shape
    books = share * slots
    block = books // lines
    piece = min(share, block)
    tile = profit_refs[0].shape[1]

    @pl.when(step == 0)
    def _():
        for core in range(CORES):
            for slot in range(slots):
                ref = weight_refs[core * slots + slot]
                for at in range(0, share, piece):
                    start = (where_ref[0] ^ slot) * share + at
                    line = start // block
                    to = (where_ref[2] ^ line) * block + (start - line * block)
                    to = pl.multiple_of(to, piece)
                    held[pl.ds(to, piece), core * rows : (core + 1) * rows] = ref[at : at + piece, :]

    spot = pl.multiple_of(step * tile, tile)
    result = dot(held[:, :rows], profit_refs[0][...])
    total[:, pl.ds(spot, tile)] = result + dot(held[:, rows:], profit_refs[1][...])

    @pl.when(step == pl.num_programs(0) - 1)
    def _():
        for line in range(lines):
            at = line * block
            value = total[at : at + block, :]
            mass = jnp.sum(held[at : at + block, :].astype(F32), axis=1, keepdims=True)
            to = (line // 2 - 1) * block
            if line == 0:
                put_plain(own_ref, value, mass)
            elif line == 1:
                put_words(partner_ref, value, mass)
            elif line % 2 == 0:
                put_words(away_ref.at[to : to + block], value, mass)
            else:
                put_plain(handled_ref.at[to : to + block], value, mass)


def tail_sums(where, weights, profit_pair, slots, lines, tile):
    share, rows = weights[0].shape
    cols = profit_pair[0].shape[1]
    books = share * slots
    block = books // lines
    others = lines // 2 - 1
    wide = cols + LANES
    specs = [pl.BlockSpec((share, rows), lambda n, w: (0, 0)) for _ in weights]
    specs += [pl.BlockSpec((rows, tile), lambda n, w: (0, n)) for _ in profit_pair]
    shapes = [
        ((others * block, wide), jnp.int16),
        ((block, wide), jnp.int16),
        ((others * block, wide), F32),
        ((block, wide), F32),
    ]
    return pl.pallas_call(
        functools.partial(tail_kernel, slots, lines),
        out_shape=[jax.ShapeDtypeStruct(*shape) for shape in shapes],
        grid_spec=pltpu.PrefetchScalarGridSpec(
            num_scalar_prefetch=1,
            grid=(cols // tile,),
            in_specs=specs,
            out_specs=[pl.BlockSpec(shape, lambda n, w: (0, 0)) for shape, _ in shapes],
            scratch_shapes=[
                pltpu.VMEM((books, CORES * rows), BF16),
                pltpu.VMEM((books, cols), F32),
            ],
        ),
        compiler_params=params(48),
        name="tail_sums",
    )(where, *weights, *profit_pair)


def relay_kernel(words_ref, plain_ref, out_ref):
    total, mass = get_words(words_ref)
    own_total, own_mass = get_plain(plain_ref)
    put_words(out_ref, total + own_total, mass + own_mass)


def relay(words, plain):
    return pl.pallas_call(
        relay_kernel,
        out_shape=jax.ShapeDtypeStruct(words.shape, jnp.int16),
        compiler_params=params(16),
        name="relay",
    )(words, plain)


def finish_kernel(where_ref, plain_ref, *refs):
    words_refs, (keep_ref, give_ref, held) = refs[:-3], refs[-3:]
    total, mass = get_plain(plain_ref)
    for words_ref in words_refs:
        more, more_mass = get_words(words_ref)
        total, mass = total + more, mass + more_mass
    held[...] = total / mass
    rows = keep_ref.shape[0]
    keep_ref[...] = held[pl.ds(pl.multiple_of(where_ref[1] * rows, rows), rows), :]
    give_ref[...] = held[pl.ds(pl.multiple_of((1 - where_ref[1]) * rows, rows), rows), :]


def finish(where, plain, words):
    block, wide = plain.shape
    cols = wide - LANES
    vmem = pl.BlockSpec(memory_space=pltpu.VMEM)
    return pl.pallas_call(
        finish_kernel,
        out_shape=[jax.ShapeDtypeStruct((block // CORES, cols), F32)] * 2,
        in_specs=[pl.BlockSpec(memory_space=pltpu.SMEM)] + [vmem] * (1 + len(words)),
        out_specs=[vmem] * 2,
        scratch_shapes=[pltpu.VMEM((block, cols), F32)],
        compiler_params=params(16),
        name="finish",
    )(where, plain, *words)


def body(shocks, loadings, delta, gamma, kappa, book_of, bracket_low, bracket_high, rank):
    inst_cols = loadings.shape[1]
    books = bracket_low.shape[0]
    slots = lax.axis_size("inst")
    lines = lax.axis_size("scen") // CORES
    share = books // slots
    scale = (books / (inst_cols * slots)) ** 0.5
    inst = lax.axis_index("inst")
    scen = lax.axis_index("scen")
    core, line = scen % CORES, scen // CORES
    where = jnp.stack([inst, core, line]).astype(jnp.int32)

    mine, theirs, *sums = gather_and_revalue(
        where,
        shocks,
        loadings,
        delta[None, :],
        gamma[None, :],
        kappa[None, :],
        book_of[None, :],
        books,
    )
    got = swap(theirs, "scen", 1)

    own = lambda v: lax.dynamic_slice_in_dim(v, inst * share, share, 0)[:, None]
    low, high, own_rank = own(bracket_low), own(bracket_high), own(rank)
    parts = [sums[0]] + [swap(sums[slot], "inst", slot) for slot in range(1, slots)]
    value, code = book_values(scale, low, high, parts)
    codes = [code] + [swap(code, "scen", CORES * k) for k in range(1, lines)]
    codes = codes + [swap(c, "scen", 1) for c in codes]
    weight, quantile = quantiles(low, high, own_rank, value, codes)
    weights = [weight] + [swap(weight, "inst", slot) for slot in range(1, slots)]
    others = [swap(w, "scen", 1) for w in weights]

    away, partner, handled, plain = tail_sums(where, weights + others, [mine, got], slots, lines, 512)
    passed = swap(away, "scen", CORES)
    from_partner = swap(partner, "scen", CORES)
    sent = relay(passed, handled)
    block = books // lines
    words = [from_partner]
    for k in range(1, lines // 2):
        words.append(swap(sent[(k - 1) * block : k * block], "scen", CORES * (2 * k + 1)))
    keep, give = finish(where, plain, words)
    taken = swap(give, "scen", 1)
    left = jnp.where(core == 0, keep, taken)
    right = jnp.where(core == 0, taken, keep)
    return jnp.concatenate([left, right], axis=1), quantile[:, 0]


def solution(mesh):
    placed = (
        P("scen", "inst"),
        P(None, "inst"),
        P("inst"),
        P("inst"),
        P("inst"),
        P("inst"),
        P(),
        P(),
        P(),
    )
    return jax.shard_map(
        body, mesh=mesh, in_specs=placed, out_specs=(P("scen", "inst"), P("inst")), check_vma=False
    )
```

```python
import functools

import jax
import jax.numpy as jnp
from jax import lax
from jax.experimental import pallas as pl
from jax.experimental.pallas import tpu as pltpu
from jax.sharding import PartitionSpec as P

PIVOTS = 64
ROUNDS = 3
CORES = 2
LANES = 128

tail_width = 0.5
bracket_unit = 0.125
code_top = 65535.0
code_mid = 32768.0
top16 = 32600.0
octave = 0.6931471805599453
finest = 8.0
half_word = 16384.0

BF16 = jnp.bfloat16
F32 = jnp.float32


def params(megabytes):
    return pltpu.CompilerParams(vmem_limit_bytes=megabytes * 2**20)


def dot(a, b):
    return jnp.dot(a, b, preferred_element_type=F32)


def dot_nt(a, b):
    return lax.dot_general(a, b, (((1,), (1,)), ((), ())), preferred_element_type=F32)


def swap(value, axis, flip):
    n = lax.axis_size(axis)
    return lax.ppermute(value, axis, [(k, k ^ flip) for k in range(n)])


def tiles(width, tile):
    return [slice(at, at + tile) for at in range(0, width, tile)]


def stage_kernel(slots, near, far, where_ref, shocks_ref, book_ref, loadings_ref, first_ref, near_ref, far_ref, onehot_ref, own, sems):
    depth = shocks_ref.shape[1]
    books, cols = onehot_ref.shape
    share = books // slots
    rows_of = lambda flip: pl.ds(pl.multiple_of((where_ref[0] ^ flip) * depth, depth), depth)
    parts = tiles(cols, cols // 4)
    own_copies = [
        pltpu.make_async_copy(loadings_ref.at[rows_of(0), part], own.at[:, part], sems.at[k])
        for k, part in enumerate(parts)
    ]
    rest_copies = [
        pltpu.make_async_copy(
            loadings_ref.at[rows_of(flip), :],
            ref.at[k * depth : (k + 1) * depth, :],
            sems.at[len(parts) + flip - 1],
        )
        for ref, flips in ((near_ref, near), (far_ref, far))
        for k, flip in enumerate(flips)
    ]
    for copy in own_copies + rest_copies:
        copy.start()
    tile = cols // 8
    row = lax.broadcasted_iota(jnp.int32, (books, tile), 0)
    row = ((row // share) ^ where_ref[0]) * share + row % share
    for part in tiles(cols, tile):
        onehot_ref[:, part] = jnp.where(row == book_ref[:, part], 1.0, 0.0).astype(BF16)
    for copy, part in zip(own_copies, parts):
        copy.wait()
        first_ref[:, part] = dot(shocks_ref[...], own[:, part])
    for copy in rest_copies:
        copy.wait()


def stage(where, shocks, book_of, loadings, slots, near, far, books):
    rows, depth = shocks.shape
    cols = loadings.shape[1]
    vmem = pl.BlockSpec(memory_space=pltpu.VMEM)
    return pl.pallas_call(
        functools.partial(stage_kernel, slots, near, far),
        out_shape=[
            jax.ShapeDtypeStruct((rows, cols), F32),
            jax.ShapeDtypeStruct((len(near) * depth, cols), BF16),
            jax.ShapeDtypeStruct((len(far) * depth, cols), BF16),
            jax.ShapeDtypeStruct((books, cols), BF16),
        ],
        in_specs=[pl.BlockSpec(memory_space=pltpu.SMEM), vmem, vmem, pl.BlockSpec(memory_space=pltpu.HBM)],
        out_specs=[vmem] * 4,
        scratch_shapes=[pltpu.VMEM((depth, cols), BF16), pltpu.SemaphoreType.DMA((3 + slots,))],
        compiler_params=params(16),
        cost_estimate=pl.CostEstimate(
            flops=2 * rows * depth * cols, bytes_accessed=2 * loadings.size, transcendentals=0
        ),
        name="stage",
    )(where, shocks, book_of, loadings)


def add_moves_kernel(*refs):
    shock_refs, (rest_ref, before_ref, after_ref) = refs[:-3], refs[-3:]
    depth = shock_refs[0].shape[1]
    cols = after_ref.shape[1]
    for part in tiles(cols, cols // 8):
        total = before_ref[:, part]
        for k, shock_ref in enumerate(shock_refs):
            total = total + dot(shock_ref[...], rest_ref[k * depth : (k + 1) * depth, part])
        after_ref[:, part] = total


def add_moves(shocks, rest, before):
    vmem = pl.BlockSpec(memory_space=pltpu.VMEM)
    rows, cols = before.shape
    depth = shocks[0].shape[1]
    return pl.pallas_call(
        add_moves_kernel,
        out_shape=jax.ShapeDtypeStruct((rows, cols), F32),
        in_specs=[vmem] * (len(shocks) + 2),
        out_specs=vmem,
        input_output_aliases={len(shocks) + 1: 0},
        compiler_params=params(16),
        cost_estimate=pl.CostEstimate(
            flops=2 * rows * depth * cols * len(shocks), bytes_accessed=8 * rows * cols, transcendentals=0
        ),
        name="add_moves",
    )(*shocks, rest, before)


def profit_kernel(count, where_ref, *refs):
    top_refs, low_refs = refs[:count], refs[count : 2 * count]
    rest_ref, first_ref, delta_ref, gamma_ref, kappa_ref, onehot_ref = refs[2 * count : 2 * count + 6]
    mine_ref, theirs_ref = refs[2 * count + 6 : 2 * count + 8]
    sum_refs, total = refs[2 * count + 8 : -1], refs[-1]
    half, depth = top_refs[0].shape
    part_cols = mine_ref.shape[1]
    tile = part_cols // 4
    share = sum_refs[0].shape[0]
    fresh = True
    for side, out_ref in ((1 - where_ref[1], theirs_ref), (where_ref[1], mine_ref)):
        for spot in tiles(part_cols, tile):
            part = pl.ds(pl.multiple_of(side * part_cols + spot.start, tile), tile)
            pieces = []
            for at, shock_refs in ((0, top_refs), (half, low_refs)):
                moves = first_ref[at : at + half, part]
                for k, shock_ref in enumerate(shock_refs):
                    moves = moves + dot(shock_ref[...], rest_ref[k * depth : (k + 1) * depth, part])
                value = moves * (delta_ref[:, part] + moves * (gamma_ref[:, part] + moves * kappa_ref[:, part]))
                pieces.append(value.astype(BF16))
            profit = jnp.concatenate(pieces, axis=0)
            out_ref[:, spot] = profit
            sums = dot_nt(onehot_ref[:, part], profit)
            total[...] = sums if fresh else total[...] + sums
            fresh = False
    for slot, sum_ref in enumerate(sum_refs):
        sum_ref[...] = total[slot * share : (slot + 1) * share, :]


def profits(where, tops, lows, rest, first, delta, gamma, kappa, onehot, slots):
    rows, cols = first.shape
    books = onehot.shape[0]
    depth = tops[0].shape[1]
    vmem = pl.BlockSpec(memory_space=pltpu.VMEM)
    out_shape = [jax.ShapeDtypeStruct((rows, cols // CORES), BF16)] * 2
    out_shape += [jax.ShapeDtypeStruct((books // slots, rows), F32)] * slots
    return pl.pallas_call(
        functools.partial(profit_kernel, len(tops)),
        out_shape=out_shape,
        in_specs=[pl.BlockSpec(memory_space=pltpu.SMEM)] + [vmem] * (2 * len(tops) + 6),
        out_specs=[vmem] * len(out_shape),
        scratch_shapes=[pltpu.VMEM((books, rows), F32)],
        compiler_params=params(16),
        cost_estimate=pl.CostEstimate(
            flops=2 * rows * cols * (depth * len(tops) + books),
            bytes_accessed=6 * rows * cols,
            transcendentals=0,
        ),
        name="profits",
    )(where, *tops, *lows, rest, first, delta, gamma, kappa, onehot)


def gather_and_revalue(where, shocks, loadings, delta, gamma, kappa, book_of, books):
    slots = lax.axis_size("inst")
    inner = 1
    while inner * inner * 4 <= slots:
        inner *= 2
    outer = slots // inner
    half = shocks.shape[0] // 2
    along = [f for f in range(1, inner)]
    across = [f * inner for f in range(1, outer)]
    corners = [(a, b) for a in along for b in across]
    near = {f: swap(shocks, "inst", f) for f in along + across}
    first, near_loads, far_loads, onehot = stage(
        where, shocks, book_of, loadings, slots, along + across, [a ^ b for a, b in corners], books
    )
    tops = [swap(near[a][:half], "inst", b) for a, b in corners]
    lows = [swap(near[b][half:], "inst", a) for a, b in corners]
    first = add_moves([near[f] for f in along + across], near_loads, first)
    return profits(where, tops, lows, far_loads, first, delta, gamma, kappa, onehot, slots)


def book_value_kernel(scale, low_ref, high_ref, *refs):
    part_refs, (value_ref, code_ref) = refs[:-2], refs[-2:]
    value = part_refs[0][...]
    for part_ref in part_refs[1:]:
        value = value + part_ref[...]
    value = value * scale
    value_ref[...] = value
    low = low_ref[...].astype(F32) * bracket_unit
    high = high_ref[...].astype(F32) * bracket_unit
    code = (value - low) * (code_top / (high - low))
    code = jnp.minimum(jnp.maximum(code, 0.0), code_top)
    code_ref[...] = (jnp.round(code) - code_mid).astype(jnp.int32).astype(jnp.int16)


def book_values(scale, low, high, parts):
    share, rows = parts[0].shape
    return pl.pallas_call(
        functools.partial(book_value_kernel, scale),
        out_shape=[
            jax.ShapeDtypeStruct((share, rows), F32),
            jax.ShapeDtypeStruct((share, rows), jnp.int16),
        ],
        compiler_params=params(16),
        name="book_values",
    )(low, high, *parts)


def quantile_kernel(low_ref, high_ref, rank_ref, value_ref, *refs):
    code_refs, (weight_ref, quantile_ref, held) = refs[:-3], refs[-3:]
    share, rows = code_refs[0].shape
    for at, code_ref in enumerate(code_refs):
        held[:, at * rows : (at + 1) * rows] = code_ref[...].astype(F32)
    width = held.shape[1]
    low = low_ref[...].astype(F32) * bracket_unit
    high = high_ref[...].astype(F32) * bracket_unit
    rank = rank_ref[...].astype(F32)
    per_unit = code_top / (high - low)
    lower, upper = low, high
    for _ in range(ROUNDS):
        spacing = (upper - lower) / (PIVOTS - 1)
        below = jnp.zeros_like(low)
        stride = PIVOTS // 2
        while stride:
            pivot = lower + (below + (stride - 1)) * spacing
            mark = jnp.floor((pivot - low) * per_unit) - code_mid
            mark = jnp.broadcast_to(mark, (share, LANES))
            count = jnp.zeros((share, LANES), F32)
            for at in range(0, width, LANES):
                count = count + jnp.where(held[:, at : at + LANES] <= mark, 1.0, 0.0)
            count = jnp.sum(count, axis=1, keepdims=True)
            below = below + jnp.where(count < rank, float(stride), 0.0)
            stride //= 2
        chosen = jnp.clip(below, 1.0, float(PIVOTS - 1))
        lower, upper = lower + (chosen - 1.0) * spacing, lower + chosen * spacing
    quantile = (lower + upper) * 0.5
    weight_ref[...] = jax.nn.sigmoid((quantile - value_ref[...]) / tail_width).astype(BF16)
    quantile = jnp.broadcast_to(quantile, (share, LANES))
    square = jnp.concatenate([quantile, jnp.zeros((LANES - share, LANES), F32)], axis=0)
    quantile_ref[...] = square.T[: quantile_ref.shape[0], :]


def quantiles(low, high, rank, value, codes):
    share, rows = codes[0].shape
    return pl.pallas_call(
        quantile_kernel,
        out_shape=[
            jax.ShapeDtypeStruct((share, rows), BF16),
            jax.ShapeDtypeStruct((8, LANES), F32),
        ],
        scratch_shapes=[pltpu.VMEM((share, rows * len(codes)), F32)],
        compiler_params=params(16),
        name="quantiles",
    )(low, high, rank, value, *codes)


def encode(total, mass):
    top = jnp.maximum(jnp.max(jnp.abs(total), axis=1, keepdims=True), 1e-30)
    level = jnp.ceil(jnp.log(top * (1.0 / top16)) * (finest / octave))
    words = jnp.round(total * jnp.exp(level * (-octave / finest)))
    mass = jnp.maximum(mass, 1e-30)
    power = jnp.ceil(jnp.log(mass) * (1.0 / octave))
    scaled = mass * jnp.exp(power * -octave) * half_word
    upper = jnp.floor(scaled)
    lower = jnp.round((scaled - upper) * half_word)
    column = lax.broadcasted_iota(jnp.int32, (total.shape[0], LANES), 1)
    side = jnp.where(column == 0, level, 0.0)
    side = jnp.where(column == 1, power, side)
    side = jnp.where(column == 2, upper, side)
    side = jnp.where(column == 3, lower, side)
    return words.astype(jnp.int32).astype(jnp.int16), side.astype(jnp.int32).astype(jnp.int16)


def put_words(ref, total, mass):
    words, side = encode(total, mass)
    cols = total.shape[1]
    ref[:, :cols] = words
    ref[:, cols:] = side


def get_words(ref):
    cols = ref.shape[1] - LANES
    side = ref[:, cols:].astype(F32)
    level, power, upper, lower = (side[:, k : k + 1] for k in range(4))
    mass = (upper + lower * (1.0 / half_word)) * (1.0 / half_word) * jnp.exp(power * octave)
    total = ref[:, :cols].astype(F32) * jnp.exp(level * (octave / finest))
    return total, mass


def get_plain(ref):
    cols = ref.shape[1] - LANES
    return ref[:, :cols], ref[:, cols : cols + 1]


def tail_kernel(slots, lines, where_ref, *refs):
    count = CORES * slots
    weight_refs, profit_refs = refs[:count], refs[count : count + CORES]
    out_refs, (held, total) = refs[count + CORES : -2], refs[-2:]
    away_refs, partner_refs, handled_refs, own_refs = (out_refs[k : k + 2] for k in range(0, 8, 2))
    share, rows = weight_refs[0].shape
    books = share * slots
    block = books // lines
    piece = min(share, block)
    for slot in range(slots):
        for core in range(CORES):
            ref = weight_refs[core * slots + slot]
            for at in range(0, share, piece):
                start = (where_ref[0] ^ slot) * share + at
                line = start // block
                to = (where_ref[2] ^ line) * block + (start - line * block)
                to = pl.multiple_of(to, piece)
                held[pl.ds(to, piece), core * rows : (core + 1) * rows] = ref[at : at + piece, :]
    cols = total.shape[1] - LANES
    for part in tiles(cols, cols // 4):
        result = dot(held[:, :rows], profit_refs[0][:, part])
        total[:, part] = result + dot(held[:, rows:], profit_refs[1][:, part])
    mass = jnp.sum(held[...].astype(F32), axis=1, keepdims=True)
    total[:, cols:] = jnp.broadcast_to(mass, (books, LANES))
    half = block // CORES
    for side in range(CORES):
        core = where_ref[1] if side == 0 else 1 - where_ref[1]
        for line in [*range(2, lines, 2), 1, *range(3, lines, 2), 0]:
            spot = pl.ds(pl.multiple_of(line * block + core * half, half), half)
            value = total[spot, :]
            to = slice((line // 2 - 1) * half, line // 2 * half)
            if line == 0:
                own_refs[side][...] = value
            elif line == 1:
                put_words(partner_refs[side], value[:, :cols], value[:, cols : cols + 1])
            elif line % 2 == 0:
                put_words(away_refs[side].at[to, :], value[:, :cols], value[:, cols : cols + 1])
            else:
                handled_refs[side][to, :] = value


def tail_sums(where, weights, profit_pair, slots, lines):
    share, rows = weights[0].shape
    cols = profit_pair[0].shape[1]
    books = share * slots
    half = books // lines // CORES
    others = lines // 2 - 1
    wide = cols + LANES
    kinds = [(others * half, jnp.int16), (half, jnp.int16), (others * half, F32), (half, F32)]
    vmem = pl.BlockSpec(memory_space=pltpu.VMEM)
    inputs = [*weights, *profit_pair]
    return pl.pallas_call(
        functools.partial(tail_kernel, slots, lines),
        out_shape=[jax.ShapeDtypeStruct((n, wide), kind) for n, kind in kinds for _ in range(CORES)],
        in_specs=[pl.BlockSpec(memory_space=pltpu.SMEM)] + [vmem] * len(inputs),
        out_specs=[vmem] * (len(kinds) * CORES),
        scratch_shapes=[pltpu.VMEM((books, CORES * rows), BF16), pltpu.VMEM((books, wide), F32)],
        compiler_params=params(24),
        name="tail_sums",
    )(where, *inputs)


def relay_kernel(words_ref, plain_ref, out_ref):
    total, mass = get_words(words_ref)
    own_total, own_mass = get_plain(plain_ref)
    put_words(out_ref, total + own_total, mass + own_mass)


def relay(words, plain):
    return pl.pallas_call(
        relay_kernel,
        out_shape=jax.ShapeDtypeStruct(words.shape, jnp.int16),
        compiler_params=params(16),
        name="relay",
    )(words, plain)


def finish_kernel(where_ref, *refs):
    groups, out_ref = (refs[: len(refs) // 2], refs[len(refs) // 2 : -1]), refs[-1]
    cols = groups[0][0].shape[1] - LANES
    for side, group in enumerate(groups):
        total, mass = get_plain(group[0])
        for words_ref in group[1:]:
            more, more_mass = get_words(words_ref)
            total, mass = total + more, mass + more_mass
        core = where_ref[1] if side == 0 else 1 - where_ref[1]
        out_ref[:, pl.ds(pl.multiple_of(core * cols, cols), cols)] = total * (1.0 / mass)


def finish(where, groups):
    half, wide = groups[0][0].shape
    inputs = [*groups[0], *groups[1]]
    vmem = pl.BlockSpec(memory_space=pltpu.VMEM)
    return pl.pallas_call(
        finish_kernel,
        out_shape=jax.ShapeDtypeStruct((half, (wide - LANES) * CORES), F32),
        in_specs=[pl.BlockSpec(memory_space=pltpu.SMEM)] + [vmem] * len(inputs),
        out_specs=vmem,
        compiler_params=params(16),
        name="finish",
    )(where, *inputs)


def body(shocks, loadings, delta, gamma, kappa, book_of, bracket_low, bracket_high, rank):
    inst_cols = loadings.shape[1]
    books = bracket_low.shape[0]
    slots = lax.axis_size("inst")
    lines = lax.axis_size("scen") // CORES
    share = books // slots
    scale = (books / (inst_cols * slots)) ** 0.5
    inst = lax.axis_index("inst")
    scen = lax.axis_index("scen")
    core, line = scen % CORES, scen // CORES
    where = jnp.stack([inst, core, line]).astype(jnp.int32)

    mine, theirs, *sums = gather_and_revalue(
        where,
        shocks,
        loadings,
        delta[None, :],
        gamma[None, :],
        kappa[None, :],
        book_of[None, :],
        books,
    )
    got = swap(theirs, "scen", 1)

    own = lambda v: lax.dynamic_slice_in_dim(v, inst * share, share, 0)[:, None]
    low, high, own_rank = own(bracket_low), own(bracket_high), own(rank)
    parts = [sums[0]] + [swap(sums[slot], "inst", slot) for slot in range(1, slots)]
    value, code = book_values(scale, low, high, parts)
    codes = [code] + [swap(code, "scen", CORES * k) for k in range(1, lines)]
    codes = codes + [swap(c, "scen", 1) for c in codes]
    weight, row = quantiles(low, high, own_rank, value, codes)
    weights = [weight] + [swap(weight, "inst", slot) for slot in range(1, slots)]
    weights = weights + [swap(w, "scen", 1) for w in weights]

    outs = tail_sums(where, weights, [mine, got], slots, lines)
    away, partner, handled, plain = (outs[k : k + 2] for k in range(0, 8, 2))
    half = books // lines // CORES
    groups = []
    for side in range(CORES):
        passed = swap(away[side], "scen", CORES)
        words = [swap(partner[side], "scen", CORES ^ side)]
        sent = relay(passed, handled[side])
        for k in range(1, lines // 2):
            block = sent[(k - 1) * half : k * half]
            words.append(swap(block, "scen", (CORES * (2 * k + 1)) ^ side))
        first = plain[0] if side == 0 else swap(plain[1], "scen", 1)
        groups.append([first, *words])
    return finish(where, groups), row[0, :share]


def solution(mesh):
    placed = (
        P("scen", "inst"),
        P(None, "inst"),
        P("inst"),
        P("inst"),
        P("inst"),
        P("inst"),
        P(),
        P(),
        P(),
    )
    return jax.shard_map(
        body, mesh=mesh, in_specs=placed, out_specs=(P("scen", "inst"), P("inst")), check_vma=False
    )
```

```python
import functools

import jax
import jax.numpy as jnp
from jax import lax
from jax.experimental import pallas as pl
from jax.experimental.pallas import tpu as pltpu
from jax.sharding import PartitionSpec as P

PIVOTS = 64
ROUNDS = 3
CORES = 2
LANES = 128
RANK_PART = 64

tail_width = 0.5
bracket_unit = 0.125
top16 = 32600.0
octave = 0.6931471805599453
finest = 8.0
half_word = 16384.0

BF16 = jnp.bfloat16
F32 = jnp.float32


def params(megabytes):
    return pltpu.CompilerParams(vmem_limit_bytes=megabytes * 2**20)


def dot(a, b):
    return jnp.dot(a, b, preferred_element_type=F32)


def dot_nt(a, b):
    return lax.dot_general(a, b, (((1,), (1,)), ((), ())), preferred_element_type=F32)


def swap(value, axis, flip):
    n = lax.axis_size(axis)
    return lax.ppermute(value, axis, [(k, k ^ flip) for k in range(n)])


def tiles(width, tile):
    return [slice(at, at + tile) for at in range(0, width, tile)]


def stage_kernel(slots, near, far, where_ref, shocks_ref, book_ref, loadings_ref, first_ref, near_ref, far_ref, onehot_ref, own, sems):
    depth = shocks_ref.shape[1]
    books, cols = onehot_ref.shape
    share = books // slots
    rows_of = lambda flip: pl.ds(pl.multiple_of((where_ref[0] ^ flip) * depth, depth), depth)
    parts = tiles(cols, cols // 4)
    own_copies = [
        pltpu.make_async_copy(loadings_ref.at[rows_of(0), part], own.at[:, part], sems.at[k])
        for k, part in enumerate(parts)
    ]
    rest_copies = [
        pltpu.make_async_copy(
            loadings_ref.at[rows_of(flip), :],
            ref.at[k * depth : (k + 1) * depth, :],
            sems.at[len(parts) + flip - 1],
        )
        for ref, flips in ((near_ref, near), (far_ref, far))
        for k, flip in enumerate(flips)
    ]
    for copy in own_copies + rest_copies:
        copy.start()
    tile = cols // 8
    row = lax.broadcasted_iota(jnp.int32, (books, tile), 0)
    row = ((row // share) ^ where_ref[0]) * share + row % share
    for part in tiles(cols, tile):
        onehot_ref[:, part] = jnp.where(row == book_ref[:, part], 1.0, 0.0).astype(BF16)
    for copy, part in zip(own_copies, parts):
        copy.wait()
        first_ref[:, part] = dot(shocks_ref[...], own[:, part])
    for copy in rest_copies:
        copy.wait()


def stage(where, shocks, book_of, loadings, slots, near, far, books):
    rows, depth = shocks.shape
    cols = loadings.shape[1]
    vmem = pl.BlockSpec(memory_space=pltpu.VMEM)
    return pl.pallas_call(
        functools.partial(stage_kernel, slots, near, far),
        out_shape=[
            jax.ShapeDtypeStruct((rows, cols), F32),
            jax.ShapeDtypeStruct((len(near) * depth, cols), BF16),
            jax.ShapeDtypeStruct((len(far) * depth, cols), BF16),
            jax.ShapeDtypeStruct((books, cols), BF16),
        ],
        in_specs=[pl.BlockSpec(memory_space=pltpu.SMEM), vmem, vmem, pl.BlockSpec(memory_space=pltpu.HBM)],
        out_specs=[vmem] * 4,
        scratch_shapes=[pltpu.VMEM((depth, cols), BF16), pltpu.SemaphoreType.DMA((3 + slots,))],
        compiler_params=params(16),
        cost_estimate=pl.CostEstimate(
            flops=2 * rows * depth * cols, bytes_accessed=2 * loadings.size, transcendentals=0
        ),
        name="stage",
    )(where, shocks, book_of, loadings)


def add_moves_kernel(*refs):
    shock_refs, (rest_ref, before_ref, after_ref) = refs[:-3], refs[-3:]
    depth = shock_refs[0].shape[1]
    cols = after_ref.shape[1]
    for part in tiles(cols, cols // 8):
        total = before_ref[:, part]
        for k, shock_ref in enumerate(shock_refs):
            total = total + dot(shock_ref[...], rest_ref[k * depth : (k + 1) * depth, part])
        after_ref[:, part] = total


def add_moves(shocks, rest, before):
    vmem = pl.BlockSpec(memory_space=pltpu.VMEM)
    rows, cols = before.shape
    depth = shocks[0].shape[1]
    return pl.pallas_call(
        add_moves_kernel,
        out_shape=jax.ShapeDtypeStruct((rows, cols), F32),
        in_specs=[vmem] * (len(shocks) + 2),
        out_specs=vmem,
        input_output_aliases={len(shocks) + 1: 0},
        compiler_params=params(16),
        cost_estimate=pl.CostEstimate(
            flops=2 * rows * depth * cols * len(shocks), bytes_accessed=8 * rows * cols, transcendentals=0
        ),
        name="add_moves",
    )(*shocks, rest, before)


def profit_kernel(count, where_ref, *refs):
    top_refs, low_refs = refs[:count], refs[count : 2 * count]
    rest_ref, first_ref, delta_ref, gamma_ref, kappa_ref, onehot_ref = refs[2 * count : 2 * count + 6]
    mine_ref, theirs_ref = refs[2 * count + 6 : 2 * count + 8]
    sum_refs, (total, held, sems) = refs[2 * count + 8 : -3], refs[-3:]
    half, depth = top_refs[0].shape
    part_cols = mine_ref.shape[1]
    tile = part_cols // 4
    share = sum_refs[0].shape[0]
    fresh, copies = True, []
    for side, out_ref in ((1 - where_ref[1], held), (where_ref[1], mine_ref)):
        for spot in tiles(part_cols, tile):
            part = pl.ds(pl.multiple_of(side * part_cols + spot.start, tile), tile)
            pieces = []
            for at, shock_refs in ((0, top_refs), (half, low_refs)):
                moves = first_ref[at : at + half, part]
                for k, shock_ref in enumerate(shock_refs):
                    moves = moves + dot(shock_ref[...], rest_ref[k * depth : (k + 1) * depth, part])
                value = moves * (delta_ref[:, part] + moves * (gamma_ref[:, part] + moves * kappa_ref[:, part]))
                pieces.append(value.astype(BF16))
            profit = jnp.concatenate(pieces, axis=0)
            out_ref[:, spot] = profit
            if out_ref is held:
                copies.append(pltpu.make_async_copy(held.at[:, spot], theirs_ref.at[:, spot], sems.at[len(copies)]))
                copies[-1].start()
            sums = dot_nt(onehot_ref[:, part], profit)
            total[...] = sums if fresh else total[...] + sums
            fresh = False
    for slot, sum_ref in enumerate(sum_refs):
        sum_ref[...] = total[slot * share : (slot + 1) * share, :]
    for copy in copies:
        copy.wait()


def profits(where, tops, lows, rest, first, delta, gamma, kappa, onehot, slots):
    rows, cols = first.shape
    books = onehot.shape[0]
    depth = tops[0].shape[1]
    vmem = pl.BlockSpec(memory_space=pltpu.VMEM)
    out_shape = [jax.ShapeDtypeStruct((rows, cols // CORES), BF16)] * 2
    out_shape += [jax.ShapeDtypeStruct((books // slots, rows), F32)] * slots
    return pl.pallas_call(
        functools.partial(profit_kernel, len(tops)),
        out_shape=out_shape,
        in_specs=[pl.BlockSpec(memory_space=pltpu.SMEM)] + [vmem] * (2 * len(tops) + 6),
        out_specs=[vmem, pl.BlockSpec(memory_space=pltpu.HBM)] + [vmem] * slots,
        scratch_shapes=[
            pltpu.VMEM((books, rows), F32),
            pltpu.VMEM((rows, cols // CORES), BF16),
            pltpu.SemaphoreType.DMA((4,)),
        ],
        compiler_params=params(16),
        cost_estimate=pl.CostEstimate(
            flops=2 * rows * cols * (depth * len(tops) + books),
            bytes_accessed=6 * rows * cols,
            transcendentals=0,
        ),
        name="profits",
    )(where, *tops, *lows, rest, first, delta, gamma, kappa, onehot)


def gather_and_revalue(where, shocks, loadings, delta, gamma, kappa, book_of, books):
    slots = lax.axis_size("inst")
    inner = 1
    while inner * inner * 4 <= slots:
        inner *= 2
    outer = slots // inner
    half = shocks.shape[0] // 2
    along = [f for f in range(1, inner)]
    across = [f * inner for f in range(1, outer)]
    corners = [(a, b) for a in along for b in across]
    near = {f: swap(shocks, "inst", f) for f in along + across}
    first, near_loads, far_loads, onehot = stage(
        where, shocks, book_of, loadings, slots, along + across, [a ^ b for a, b in corners], books
    )
    tops = [swap(near[a][:half], "inst", b) for a, b in corners]
    lows = [swap(near[b][half:], "inst", a) for a, b in corners]
    first = add_moves([near[f] for f in along + across], near_loads, first)
    return profits(where, tops, lows, far_loads, first, delta, gamma, kappa, onehot, slots)


def sorting_pairs(n):
    pairs, p = [], 1
    while p < n:
        k = p
        while k:
            for j in range(k % p, n - k, 2 * k):
                for i in range(j, j + min(k, n - j - k)):
                    if i // (2 * p) == (i + k) // (2 * p):
                        pairs.append((i, i + k))
            k //= 2
        p *= 2
    return pairs


def compare(values, pairs):
    for i, j in pairs:
        values[i], values[j] = jnp.minimum(values[i], values[j]), jnp.maximum(values[i], values[j])
    return values


def merged(one, other, most):
    n = len(one)
    if 2 * n <= most:
        values = one + other[::-1]
    else:
        values = [jnp.minimum(a, b) for a, b in zip(one, other[::-1])]
    n = len(values)
    stride = n // 2
    while stride:
        compare(values, [(i, i + stride) for i in range(n) if not i & stride])
        stride //= 2
    return values


def lowest(values, share, most):
    values = compare(list(values), sorting_pairs(len(values)))
    for axis, shift in [(0, 4), (0, 2), (0, 1)] + [(1, shift) for shift in doubling(share, LANES)]:
        values = merged(values, [pltpu.roll(v, shift, axis) for v in values], most)
    return values


def doubling(start, stop):
    while start < stop:
        yield start
        start *= 2


def blocks_of(ref):
    return [ref[at : at + 8, :] for at in range(0, ref.shape[0], 8)]


def book_value_kernel(scale, most, *refs):
    part_refs, (value_ref, list_ref) = refs[:-2], refs[-2:]
    value = part_refs[0][...]
    for part_ref in part_refs[1:]:
        value = value + part_ref[...]
    value = value * scale
    value_ref[...] = value
    share, rows = value.shape
    groups = LANES // share
    depth = rows // groups
    columns = jnp.concatenate([value[:, at : at + depth] for at in range(0, rows, depth)], axis=0).T
    values = lowest([columns[at : at + 8, :] for at in range(0, depth, 8)], share, most)
    place = lax.broadcasted_iota(jnp.int32, (8, LANES), 0)
    place = place + lax.broadcasted_iota(jnp.int32, (8, LANES), 1) // share * 8
    for at in range(0, most, 8 * groups):
        block = values[at]
        for k in range(1, 8 * groups):
            block = jnp.where(place == k, values[at + k], block)
        list_ref[at // groups : at // groups + 8, :] = block


def book_values(scale, most, parts):
    share, rows = parts[0].shape
    return pl.pallas_call(
        functools.partial(book_value_kernel, scale, most),
        out_shape=[
            jax.ShapeDtypeStruct((share, rows), F32),
            jax.ShapeDtypeStruct((most * share // LANES, LANES), F32),
        ],
        compiler_params=params(16),
        name="book_values",
    )(*parts)


def quantile_kernel(most, low_ref, high_ref, rank_ref, value_ref, *refs):
    list_refs, (weight_ref, quantile_ref) = refs[:-2], refs[-2:]
    share, rows = value_ref.shape
    values = lowest([block for ref in list_refs for block in blocks_of(ref)], share, most)
    rank = jnp.broadcast_to(rank_ref[...], (8, LANES))
    sought = values[0]
    for k in range(1, most):
        sought = jnp.where(rank > k, values[k], sought)
    sought = sought[:1, :]
    lower = low_ref[...].astype(F32) * bracket_unit
    upper = high_ref[...].astype(F32) * bracket_unit
    levels = lax.broadcasted_iota(jnp.int32, (PIVOTS, LANES), 0).astype(F32)
    for _ in range(ROUNDS):
        spacing = (upper - lower) / (PIVOTS - 1)
        below = jnp.where(lower + levels * spacing < sought, 1.0, 0.0)
        chosen = jnp.clip(jnp.sum(below, axis=0, keepdims=True), 1.0, float(PIVOTS - 1))
        lower, upper = lower + (chosen - 1.0) * spacing, lower + chosen * spacing
    quantile = (lower + upper) * 0.5
    quantile_ref[...] = jnp.broadcast_to(quantile, quantile_ref.shape)
    column = jnp.broadcast_to(quantile, (LANES, LANES)).T[:share, :]
    column = jnp.concatenate([column] * (rows // LANES), axis=1)
    weight_ref[...] = jax.nn.sigmoid((column - value_ref[...]) / tail_width).astype(BF16)


def quantiles(most, low, high, rank, value, lists):
    share, rows = value.shape
    return pl.pallas_call(
        functools.partial(quantile_kernel, most),
        out_shape=[
            jax.ShapeDtypeStruct((share, rows), BF16),
            jax.ShapeDtypeStruct((8, LANES), F32),
        ],
        compiler_params=params(16),
        name="quantiles",
    )(low, high, rank, value, *lists)


def encode(total, mass):
    top = jnp.maximum(jnp.max(jnp.abs(total), axis=1, keepdims=True), 1e-30)
    level = jnp.ceil(jnp.log(top * (1.0 / top16)) * (finest / octave))
    words = jnp.round(total * jnp.exp(level * (-octave / finest)))
    mass = jnp.maximum(mass, 1e-30)
    power = jnp.ceil(jnp.log(mass) * (1.0 / octave))
    scaled = mass * jnp.exp(power * -octave) * half_word
    upper = jnp.floor(scaled)
    lower = jnp.round((scaled - upper) * half_word)
    column = lax.broadcasted_iota(jnp.int32, (total.shape[0], LANES), 1)
    side = jnp.where(column == 0, level, 0.0)
    side = jnp.where(column == 1, power, side)
    side = jnp.where(column == 2, upper, side)
    side = jnp.where(column == 3, lower, side)
    return words.astype(jnp.int32).astype(jnp.int16), side.astype(jnp.int32).astype(jnp.int16)


def put_words(ref, total, mass):
    words, side = encode(total, mass)
    cols = total.shape[1]
    ref[:, :cols] = words
    ref[:, cols:] = side


def get_words(ref):
    cols = ref.shape[1] - LANES
    side = ref[:, cols:].astype(F32)
    level, power, upper, lower = (side[:, k : k + 1] for k in range(4))
    mass = (upper + lower * (1.0 / half_word)) * (1.0 / half_word) * jnp.exp(power * octave)
    total = ref[:, :cols].astype(F32) * jnp.exp(level * (octave / finest))
    return total, mass


def get_plain(ref):
    cols = ref.shape[1] - LANES
    return ref[:, :cols], ref[:, cols : cols + 1]


def tail_part(held, profit_refs, total, spot, rows):
    cols = total.shape[1] - LANES
    weight = held[spot, :]
    for part in tiles(cols, cols // 4):
        result = dot(weight[:, :rows], profit_refs[0][:, part])
        total[spot, part] = result + dot(weight[:, rows:], profit_refs[1][:, part])
    mass = jnp.sum(weight.astype(F32), axis=1, keepdims=True)
    total[spot, cols:] = jnp.broadcast_to(mass, (weight.shape[0], LANES))


def halves(where_ref, total, line, block):
    half = block // CORES
    for side in range(CORES):
        core = where_ref[1] if side == 0 else 1 - where_ref[1]
        value = total[pl.ds(pl.multiple_of(line * block + core * half, half), half), :]
        yield side, value


def away_kernel(slots, lines, where_ref, *refs):
    count = CORES * slots
    weight_refs, profit_refs = refs[:count], refs[count : count + CORES]
    away_refs, (held, total) = refs[count + CORES : -2], refs[-2:]
    share, rows = weight_refs[0].shape
    block = share * slots // lines
    piece = min(share, block)
    cols = total.shape[1] - LANES
    half = block // CORES
    away = [line for line in range(2, lines, 2)]
    order = away + [1] + [line for line in range(3, lines, 2)] + [0]
    for slot in range(slots):
        for core in range(CORES):
            ref = weight_refs[core * slots + slot]
            for at in range(0, share, piece):
                start = (where_ref[0] ^ slot) * share + at
                line = start // block
                flip = where_ref[2] ^ line
                place = 0
                for k, known in enumerate(order):
                    place = place + jnp.where(flip == known, k, 0)
                to = pl.multiple_of(place * block + (start - line * block), piece)
                held[pl.ds(to, piece), core * rows : (core + 1) * rows] = ref[at : at + piece, :]
    tail_part(held, profit_refs, total, slice(0, len(away) * block), rows)
    for k in range(len(away)):
        for side, value in halves(where_ref, total, k, block):
            put_words(away_refs[side].at[k * half : (k + 1) * half, :], value[:, :cols], value[:, cols : cols + 1])


def home_kernel(lines, where_ref, held, *refs):
    profit_refs, (partner_refs, handled_refs, own_refs) = refs[:CORES], (refs[k : k + 2] for k in (2, 4, 6))
    total = refs[-1]
    rows = held.shape[1] // CORES
    block = held.shape[0] // lines
    half = block // CORES
    cols = total.shape[1] - LANES
    skip = lines // 2 - 1
    tail_part(held, profit_refs, total, slice(skip * block, lines * block), rows)
    for side, value in halves(where_ref, total, skip, block):
        put_words(partner_refs[side], value[:, :cols], value[:, cols : cols + 1])
    for k in range(skip):
        for side, value in halves(where_ref, total, skip + 1 + k, block):
            handled_refs[side][k * half : (k + 1) * half, :] = value
    for side, value in halves(where_ref, total, lines - 1, block):
        own_refs[side][...] = value


def tail_call(kernel, name, out_shape, scratch, where, inputs):
    vmem = pl.BlockSpec(memory_space=pltpu.VMEM)
    return pl.pallas_call(
        kernel,
        out_shape=[jax.ShapeDtypeStruct(shape, kind) for shape, kind in out_shape],
        in_specs=[pl.BlockSpec(memory_space=pltpu.SMEM)] + [vmem] * len(inputs),
        out_specs=[vmem] * len(out_shape),
        scratch_shapes=[pltpu.VMEM(shape, kind) for shape, kind in scratch],
        compiler_params=params(24),
        name=name,
    )(where, *inputs)


def tail_sums(where, weights, profit_pair, slots, lines):
    share, rows = weights[0].shape
    cols = profit_pair[0].shape[1]
    books = share * slots
    half = books // lines // CORES
    others = (lines // 2 - 1) * half
    wide = cols + LANES
    total = ((books, wide), F32)
    held_shape = ((books, CORES * rows), BF16)
    *away, held = tail_call(
        functools.partial(away_kernel, slots, lines),
        "away_sums",
        [((others, wide), jnp.int16)] * CORES + [held_shape],
        [total],
        where,
        [*weights, *profit_pair],
    )
    kinds = [(half, jnp.int16), (others, F32), (half, F32)]
    outs = tail_call(
        functools.partial(home_kernel, lines),
        "home_sums",
        [((n, wide), kind) for n, kind in kinds for _ in range(CORES)],
        [total],
        where,
        [held, *profit_pair],
    )
    return away, outs[0:2], outs[2:4], outs[4:6]


def relay_kernel(words_ref, plain_ref, out_ref):
    total, mass = get_words(words_ref)
    own_total, own_mass = get_plain(plain_ref)
    put_words(out_ref, total + own_total, mass + own_mass)


def relay(words, plain):
    return pl.pallas_call(
        relay_kernel,
        out_shape=jax.ShapeDtypeStruct(words.shape, jnp.int16),
        compiler_params=params(16),
        name="relay",
    )(words, plain)


def merge_kernel(plain_ref, words_ref, out_ref):
    total, mass = get_plain(plain_ref)
    more, more_mass = get_words(words_ref)
    cols = total.shape[1]
    out_ref[:, :cols] = total + more
    out_ref[:, cols:] = jnp.broadcast_to(mass + more_mass, (total.shape[0], LANES))


def merge(plain, words):
    return pl.pallas_call(
        merge_kernel,
        out_shape=jax.ShapeDtypeStruct(plain.shape, F32),
        compiler_params=params(16),
        name="merge",
    )(plain, words)


def finish_kernel(where_ref, *refs):
    groups, out_ref = (refs[: len(refs) // 2], refs[len(refs) // 2 : -1]), refs[-1]
    cols = groups[0][0].shape[1] - LANES
    for side, group in enumerate(groups):
        total, mass = get_plain(group[0])
        for words_ref in group[1:]:
            more, more_mass = get_words(words_ref)
            total, mass = total + more, mass + more_mass
        core = where_ref[1] if side == 0 else 1 - where_ref[1]
        out_ref[:, pl.ds(pl.multiple_of(core * cols, cols), cols)] = total * (1.0 / mass)


def finish(where, groups):
    half, wide = groups[0][0].shape
    inputs = [*groups[0], *groups[1]]
    vmem = pl.BlockSpec(memory_space=pltpu.VMEM)
    return pl.pallas_call(
        finish_kernel,
        out_shape=jax.ShapeDtypeStruct((half, (wide - LANES) * CORES), F32),
        in_specs=[pl.BlockSpec(memory_space=pltpu.SMEM)] + [vmem] * len(inputs),
        out_specs=vmem,
        compiler_params=params(16),
        name="finish",
    )(where, *inputs)


def body(shocks, loadings, delta, gamma, kappa, book_of, bracket_low, bracket_high, rank):
    inst_cols = loadings.shape[1]
    books = bracket_low.shape[0]
    slots = lax.axis_size("inst")
    lines = lax.axis_size("scen") // CORES
    share = books // slots
    scale = (books / (inst_cols * slots)) ** 0.5
    inst = lax.axis_index("inst")
    scen = lax.axis_index("scen")
    core, line = scen % CORES, scen // CORES
    where = jnp.stack([inst, core, line]).astype(jnp.int32)

    mine, theirs, *sums = gather_and_revalue(
        where,
        shocks,
        loadings,
        delta[None, :],
        gamma[None, :],
        kappa[None, :],
        book_of[None, :],
        books,
    )
    got = swap(theirs, "scen", 1)

    most = shocks.shape[0] * lax.axis_size("scen") // RANK_PART
    own = lambda v: jnp.tile(lax.dynamic_slice_in_dim(v, inst * share, share, 0), LANES // share)[None, :]
    low, high, own_rank = own(bracket_low), own(bracket_high), own(rank)
    parts = [sums[0]] + [swap(sums[slot], "inst", slot) for slot in range(slots - 1, 0, -1)]
    value, lows = book_values(scale, most, parts)
    lists = [lows] + [swap(lows, "scen", CORES * k) for k in [*range(1, lines, 2), *range(2, lines, 2)]]
    lists = lists + [swap(v, "scen", 1) for v in lists]
    weight, row = quantiles(most, low, high, own_rank, value, lists)
    far = {slot: swap(weight, "inst", slot) for slot in range(slots - 1, 0, -1)}
    weights = [weight] + [far[slot] for slot in range(1, slots)]
    weights = weights + [swap(w, "scen", 1) for w in weights]

    away, partner, handled, plain = tail_sums(where, weights, [mine, got], slots, lines)
    half = books // lines // CORES
    groups = []
    for side in range(CORES):
        passed = swap(away[side], "scen", CORES)
        sent = relay(passed, handled[side])
        words = []
        for k in range(1, lines // 2):
            block = sent[(k - 1) * half : k * half]
            words.append(swap(block, "scen", (CORES * (2 * k + 1)) ^ side))
        first = plain[0] if side == 0 else swap(plain[1], "scen", 1)
        first = merge(first, swap(partner[side], "scen", CORES ^ side))
        groups.append([first, *words])
    return finish(where, groups), row[0, :share]


def solution(mesh):
    placed = (
        P("scen", "inst"),
        P(None, "inst"),
        P("inst"),
        P("inst"),
        P("inst"),
        P("inst"),
        P(),
        P(),
        P(),
    )
    return jax.shard_map(
        body, mesh=mesh, in_specs=placed, out_specs=(P("scen", "inst"), P("inst")), check_vma=False
    )
```

```python
import functools

import jax
import jax.numpy as jnp
from jax import lax
from jax.experimental import pallas as pl
from jax.experimental.pallas import tpu as pltpu
from jax.sharding import PartitionSpec as P

PIVOTS = 64
ROUNDS = 3
CORES = 2
LANES = 128
RANK_PART = 64

tail_width = 0.5
bracket_unit = 0.125
top16 = 32600.0
octave = 0.6931471805599453
finest = 8.0
half_word = 16384.0

BF16 = jnp.bfloat16
F32 = jnp.float32


def params(megabytes):
    return pltpu.CompilerParams(vmem_limit_bytes=megabytes * 2**20)


def dot(a, b):
    return jnp.dot(a, b, preferred_element_type=F32)


def swap(value, axis, flip):
    n = lax.axis_size(axis)
    return lax.ppermute(value, axis, [(k, k ^ flip) for k in range(n)])


def tiles(width, tile):
    return [slice(at, at + tile) for at in range(0, width, tile)]


def stage_kernel(slots, near, far, where_ref, shocks_ref, book_ref, loadings_ref, first_ref, near_ref, far_ref, onehot_ref, own, sems):
    depth = shocks_ref.shape[1]
    cols, books = onehot_ref.shape
    share = books // slots
    rows_of = lambda flip: pl.ds(pl.multiple_of((where_ref[0] ^ flip) * depth, depth), depth)
    parts = tiles(cols, cols // 4)
    own_copies = [
        pltpu.make_async_copy(loadings_ref.at[rows_of(0), part], own.at[:, part], sems.at[k])
        for k, part in enumerate(parts)
    ]
    rest_copies = [
        pltpu.make_async_copy(
            loadings_ref.at[rows_of(flip), :],
            ref.at[k * depth : (k + 1) * depth, :],
            sems.at[len(parts) + flip - 1],
        )
        for ref, flips in ((near_ref, near), (far_ref, far))
        for k, flip in enumerate(flips)
    ]
    for copy in own_copies + rest_copies:
        copy.start()
    tile = cols // 8
    lane = lax.broadcasted_iota(jnp.int32, (tile, LANES), 1)
    for part in tiles(cols, tile):
        book = jnp.broadcast_to(book_ref[:, part], (LANES, tile)).T
        for at in range(0, books, LANES):
            known = (((lane + at) // share) ^ where_ref[0]) * share + (lane + at) % share
            onehot_ref[part, at : at + LANES] = jnp.where(book == known, 1.0, 0.0).astype(BF16)
    for copy, part in zip(own_copies, parts):
        copy.wait()
        first_ref[:, part] = dot(shocks_ref[...], own[:, part])
    for copy in rest_copies:
        copy.wait()


def stage(where, shocks, book_of, loadings, slots, near, far, books):
    rows, depth = shocks.shape
    cols = loadings.shape[1]
    vmem = pl.BlockSpec(memory_space=pltpu.VMEM)
    return pl.pallas_call(
        functools.partial(stage_kernel, slots, near, far),
        out_shape=[
            jax.ShapeDtypeStruct((rows, cols), F32),
            jax.ShapeDtypeStruct((len(near) * depth, cols), BF16),
            jax.ShapeDtypeStruct((len(far) * depth, cols), BF16),
            jax.ShapeDtypeStruct((cols, books), BF16),
        ],
        in_specs=[pl.BlockSpec(memory_space=pltpu.SMEM), vmem, vmem, pl.BlockSpec(memory_space=pltpu.HBM)],
        out_specs=[vmem] * 4,
        scratch_shapes=[pltpu.VMEM((depth, cols), BF16), pltpu.SemaphoreType.DMA((3 + slots,))],
        compiler_params=params(16),
        cost_estimate=pl.CostEstimate(
            flops=2 * rows * depth * cols, bytes_accessed=2 * loadings.size, transcendentals=0
        ),
        name="stage",
    )(where, shocks, book_of, loadings)


def add_moves_kernel(*refs):
    shock_refs, (rest_ref, before_ref, after_ref) = refs[:-3], refs[-3:]
    depth = shock_refs[0].shape[1]
    cols = after_ref.shape[1]
    for part in tiles(cols, cols // 8):
        total = before_ref[:, part]
        for k, shock_ref in enumerate(shock_refs):
            total = total + dot(shock_ref[...], rest_ref[k * depth : (k + 1) * depth, part])
        after_ref[:, part] = total


def add_moves(shocks, rest, before):
    vmem = pl.BlockSpec(memory_space=pltpu.VMEM)
    rows, cols = before.shape
    depth = shocks[0].shape[1]
    return pl.pallas_call(
        add_moves_kernel,
        out_shape=jax.ShapeDtypeStruct((rows, cols), F32),
        in_specs=[vmem] * (len(shocks) + 2),
        out_specs=vmem,
        input_output_aliases={len(shocks) + 1: 0},
        compiler_params=params(16),
        cost_estimate=pl.CostEstimate(
            flops=2 * rows * depth * cols * len(shocks), bytes_accessed=8 * rows * cols, transcendentals=0
        ),
        name="add_moves",
    )(*shocks, rest, before)


def profit_kernel(count, where_ref, *refs):
    top_refs, low_refs = refs[:count], refs[count : 2 * count]
    rest_ref, first_ref, delta_ref, gamma_ref, kappa_ref, onehot_ref = refs[2 * count : 2 * count + 6]
    mine_ref, theirs_ref = refs[2 * count + 6 : 2 * count + 8]
    sum_refs, (total, held, sems) = refs[2 * count + 8 : -3], refs[-3:]
    half, depth = top_refs[0].shape
    part_cols = mine_ref.shape[1]
    tile = part_cols // 4
    share = sum_refs[0].shape[0]
    fresh, copies = True, []
    for side, out_ref in ((1 - where_ref[1], held), (where_ref[1], mine_ref)):
        for spot in tiles(part_cols, tile):
            part = pl.ds(pl.multiple_of(side * part_cols + spot.start, tile), tile)
            pieces = []
            for at, shock_refs in ((0, top_refs), (half, low_refs)):
                moves = first_ref[at : at + half, part]
                for k, shock_ref in enumerate(shock_refs):
                    moves = moves + dot(shock_ref[...], rest_ref[k * depth : (k + 1) * depth, part])
                value = moves * (delta_ref[:, part] + moves * (gamma_ref[:, part] + moves * kappa_ref[:, part]))
                pieces.append(value.astype(BF16))
            profit = jnp.concatenate(pieces, axis=0)
            out_ref[:, spot] = profit
            if out_ref is held:
                copies.append(pltpu.make_async_copy(held.at[:, spot], theirs_ref.at[:, spot], sems.at[len(copies)]))
                copies[-1].start()
            sums = dot(profit, onehot_ref[part, :])
            total[...] = sums if fresh else total[...] + sums
            fresh = False
    turned = total[...].T
    for slot, sum_ref in enumerate(sum_refs):
        sum_ref[...] = turned[slot * share : (slot + 1) * share, :]
    for copy in copies:
        copy.wait()


def profits(where, tops, lows, rest, first, delta, gamma, kappa, onehot, slots):
    rows, cols = first.shape
    books = onehot.shape[1]
    depth = tops[0].shape[1]
    vmem = pl.BlockSpec(memory_space=pltpu.VMEM)
    out_shape = [jax.ShapeDtypeStruct((rows, cols // CORES), BF16)] * 2
    out_shape += [jax.ShapeDtypeStruct((books // slots, rows), F32)] * slots
    return pl.pallas_call(
        functools.partial(profit_kernel, len(tops)),
        out_shape=out_shape,
        in_specs=[pl.BlockSpec(memory_space=pltpu.SMEM)] + [vmem] * (2 * len(tops) + 6),
        out_specs=[vmem, pl.BlockSpec(memory_space=pltpu.HBM)] + [vmem] * slots,
        scratch_shapes=[
            pltpu.VMEM((rows, books), F32),
            pltpu.VMEM((rows, cols // CORES), BF16),
            pltpu.SemaphoreType.DMA((4,)),
        ],
        compiler_params=params(16),
        cost_estimate=pl.CostEstimate(
            flops=2 * rows * cols * (depth * len(tops) + books),
            bytes_accessed=6 * rows * cols,
            transcendentals=0,
        ),
        name="profits",
    )(where, *tops, *lows, rest, first, delta, gamma, kappa, onehot)


def gather_and_revalue(where, shocks, loadings, delta, gamma, kappa, book_of, books):
    slots = lax.axis_size("inst")
    inner = 1
    while inner * inner * 4 <= slots:
        inner *= 2
    outer = slots // inner
    half = shocks.shape[0] // 2
    along = [f for f in range(1, inner)]
    across = [f * inner for f in range(1, outer)]
    corners = [(a, b) for a in along for b in across]
    near = {f: swap(shocks, "inst", f) for f in along + across}
    first, near_loads, far_loads, onehot = stage(
        where, shocks, book_of, loadings, slots, along + across, [a ^ b for a, b in corners], books
    )
    tops = [swap(near[a][:half], "inst", b) for a, b in corners]
    lows = [swap(near[b][half:], "inst", a) for a, b in corners]
    first = add_moves([near[f] for f in along + across], near_loads, first)
    return profits(where, tops, lows, far_loads, first, delta, gamma, kappa, onehot, slots)


def sorting_pairs(n):
    pairs, p = [], 1
    while p < n:
        k = p
        while k:
            for j in range(k % p, n - k, 2 * k):
                for i in range(j, j + min(k, n - j - k)):
                    if i // (2 * p) == (i + k) // (2 * p):
                        pairs.append((i, i + k))
            k //= 2
        p *= 2
    return pairs


def compare(values, pairs):
    for i, j in pairs:
        values[i], values[j] = jnp.minimum(values[i], values[j]), jnp.maximum(values[i], values[j])
    return values


def merged(one, other, most):
    n = len(one)
    if 2 * n <= most:
        values = one + other[::-1]
    else:
        values = [jnp.minimum(a, b) for a, b in zip(one, other[::-1])]
    n = len(values)
    stride = n // 2
    while stride:
        compare(values, [(i, i + stride) for i in range(n) if not i & stride])
        stride //= 2
    return values


def lowest(values, share, most):
    values = compare(list(values), sorting_pairs(len(values)))
    for axis, shift in [(0, 4), (0, 2), (0, 1)] + [(1, shift) for shift in doubling(share, LANES)]:
        values = merged(values, [pltpu.roll(v, shift, axis) for v in values], most)
    return values


def doubling(start, stop):
    while start < stop:
        yield start
        start *= 2


def blocks_of(ref):
    return [ref[at : at + 8, :] for at in range(0, ref.shape[0], 8)]


def book_value_kernel(scale, most, *refs):
    part_refs, (value_ref, list_ref) = refs[:-2], refs[-2:]
    value = part_refs[0][...]
    for part_ref in part_refs[1:]:
        value = value + part_ref[...]
    value = value * scale
    value_ref[...] = value
    share, rows = value.shape
    groups = LANES // share
    depth = rows // groups
    columns = jnp.concatenate([value[:, at : at + depth] for at in range(0, rows, depth)], axis=0).T
    values = lowest([columns[at : at + 8, :] for at in range(0, depth, 8)], share, most)
    place = lax.broadcasted_iota(jnp.int32, (8, LANES), 0)
    place = place + lax.broadcasted_iota(jnp.int32, (8, LANES), 1) // share * 8
    for at in range(0, most, 8 * groups):
        block = values[at]
        for k in range(1, 8 * groups):
            block = jnp.where(place == k, values[at + k], block)
        list_ref[at // groups : at // groups + 8, :] = block


def book_values(scale, most, parts):
    share, rows = parts[0].shape
    return pl.pallas_call(
        functools.partial(book_value_kernel, scale, most),
        out_shape=[
            jax.ShapeDtypeStruct((share, rows), F32),
            jax.ShapeDtypeStruct((most * share // LANES, LANES), F32),
        ],
        compiler_params=params(16),
        name="book_values",
    )(*parts)


def quantile_kernel(most, low_ref, high_ref, rank_ref, value_ref, *refs):
    list_refs, (weight_ref, quantile_ref) = refs[:-2], refs[-2:]
    share, rows = value_ref.shape
    values = lowest([block for ref in list_refs for block in blocks_of(ref)], share, most)
    rank = jnp.broadcast_to(rank_ref[...], (8, LANES))
    sought = values[0]
    for k in range(1, most):
        sought = jnp.where(rank > k, values[k], sought)
    sought = sought[:1, :]
    lower = low_ref[...].astype(F32) * bracket_unit
    upper = high_ref[...].astype(F32) * bracket_unit
    levels = lax.broadcasted_iota(jnp.int32, (PIVOTS, LANES), 0).astype(F32)
    for _ in range(ROUNDS):
        spacing = (upper - lower) / (PIVOTS - 1)
        below = jnp.where(lower + levels * spacing < sought, 1.0, 0.0)
        chosen = jnp.clip(jnp.sum(below, axis=0, keepdims=True), 1.0, float(PIVOTS - 1))
        lower, upper = lower + (chosen - 1.0) * spacing, lower + chosen * spacing
    quantile = (lower + upper) * 0.5
    quantile_ref[...] = jnp.broadcast_to(quantile, quantile_ref.shape)
    column = jnp.broadcast_to(quantile, (LANES, LANES)).T[:share, :]
    column = jnp.concatenate([column] * (rows // LANES), axis=1)
    weight_ref[...] = jax.nn.sigmoid((column - value_ref[...]) / tail_width).astype(BF16)


def quantiles(most, low, high, rank, value, lists):
    share, rows = value.shape
    return pl.pallas_call(
        functools.partial(quantile_kernel, most),
        out_shape=[
            jax.ShapeDtypeStruct((share, rows), BF16),
            jax.ShapeDtypeStruct((8, LANES), F32),
        ],
        compiler_params=params(16),
        name="quantiles",
    )(low, high, rank, value, *lists)


def encode(total, mass):
    top = jnp.maximum(jnp.max(jnp.abs(total), axis=1, keepdims=True), 1e-30)
    level = jnp.ceil(jnp.log(top * (1.0 / top16)) * (finest / octave))
    words = jnp.round(total * jnp.exp(level * (-octave / finest)))
    mass = jnp.maximum(mass, 1e-30)
    power = jnp.ceil(jnp.log(mass) * (1.0 / octave))
    scaled = mass * jnp.exp(power * -octave) * half_word
    upper = jnp.floor(scaled)
    lower = jnp.round((scaled - upper) * half_word)
    column = lax.broadcasted_iota(jnp.int32, (total.shape[0], LANES), 1)
    side = jnp.where(column == 0, level, 0.0)
    side = jnp.where(column == 1, power, side)
    side = jnp.where(column == 2, upper, side)
    side = jnp.where(column == 3, lower, side)
    return words.astype(jnp.int32).astype(jnp.int16), side.astype(jnp.int32).astype(jnp.int16)


def put_words(ref, total, mass):
    words, side = encode(total, mass)
    cols = total.shape[1]
    ref[:, :cols] = words
    ref[:, cols:] = side


def get_words(ref):
    cols = ref.shape[1] - LANES
    side = ref[:, cols:].astype(F32)
    level, power, upper, lower = (side[:, k : k + 1] for k in range(4))
    mass = (upper + lower * (1.0 / half_word)) * (1.0 / half_word) * jnp.exp(power * octave)
    total = ref[:, :cols].astype(F32) * jnp.exp(level * (octave / finest))
    return total, mass


def get_plain(ref):
    cols = ref.shape[1] - LANES
    return ref[:, :cols], ref[:, cols : cols + 1]


def tail_part(held, profit_refs, total, spot, rows):
    cols = total.shape[1] - LANES
    weight = held[spot, :]
    mass = jnp.sum(weight.astype(F32), axis=1, keepdims=True)
    total[spot, cols:] = jnp.broadcast_to(mass, (weight.shape[0], LANES))
    for part in tiles(cols, cols // 4):
        result = dot(weight[:, :rows], profit_refs[0][:, part])
        total[spot, part] = result + dot(weight[:, rows:], profit_refs[1][:, part])


def halves(where_ref, total, line, block):
    half = block // CORES
    for side in range(CORES):
        core = where_ref[1] if side == 0 else 1 - where_ref[1]
        value = total[pl.ds(pl.multiple_of(line * block + core * half, half), half), :]
        yield side, value


def away_kernel(slots, lines, where_ref, *refs):
    count = CORES * slots
    weight_refs, profit_refs = refs[:count], refs[count : count + CORES]
    away_refs, (held, total) = refs[count + CORES : -2], refs[-2:]
    share, rows = weight_refs[0].shape
    block = share * slots // lines
    piece = min(share, block)
    cols = total.shape[1] - LANES
    half = block // CORES
    away = [line for line in range(2, lines, 2)]
    order = away + [1] + [line for line in range(3, lines, 2)] + [0]
    for slot in range(slots):
        for core in range(CORES):
            ref = weight_refs[core * slots + slot]
            for at in range(0, share, piece):
                start = (where_ref[0] ^ slot) * share + at
                line = start // block
                flip = where_ref[2] ^ line
                place = 0
                for k, known in enumerate(order):
                    place = place + jnp.where(flip == known, k, 0)
                to = pl.multiple_of(place * block + (start - line * block), piece)
                held[pl.ds(to, piece), core * rows : (core + 1) * rows] = ref[at : at + piece, :]
    tail_part(held, profit_refs, total, slice(0, len(away) * block), rows)
    for k in range(len(away)):
        for side, value in halves(where_ref, total, k, block):
            put_words(away_refs[side].at[k * half : (k + 1) * half, :], value[:, :cols], value[:, cols : cols + 1])


def home_kernel(lines, where_ref, held, *refs):
    profit_refs, (partner_refs, handled_refs, own_refs) = refs[:CORES], (refs[k : k + 2] for k in (2, 4, 6))
    total = refs[-1]
    rows = held.shape[1] // CORES
    block = held.shape[0] // lines
    half = block // CORES
    cols = total.shape[1] - LANES
    skip = lines // 2 - 1
    tail_part(held, profit_refs, total, slice(skip * block, lines * block), rows)
    for side, value in halves(where_ref, total, skip, block):
        put_words(partner_refs[side], value[:, :cols], value[:, cols : cols + 1])
    for k in range(skip):
        for side, value in halves(where_ref, total, skip + 1 + k, block):
            handled_refs[side][k * half : (k + 1) * half, :] = value
    for side, value in halves(where_ref, total, lines - 1, block):
        own_refs[side][...] = value


def bring_kernel(far_ref, near_ref, sem):
    copy = pltpu.make_async_copy(far_ref, near_ref, sem)
    copy.start()
    copy.wait()


def bring(far):
    return pl.pallas_call(
        bring_kernel,
        out_shape=jax.ShapeDtypeStruct(far.shape, far.dtype),
        in_specs=[pl.BlockSpec(memory_space=pltpu.HBM)],
        out_specs=pl.BlockSpec(memory_space=pltpu.VMEM),
        scratch_shapes=[pltpu.SemaphoreType.DMA],
        compiler_params=params(16),
        cost_estimate=pl.CostEstimate(flops=0, bytes_accessed=8 * far.size, transcendentals=0),
        name="bring",
    )(far)


def tail_call(kernel, name, out_shape, scratch, where, inputs):
    vmem = pl.BlockSpec(memory_space=pltpu.VMEM)
    return pl.pallas_call(
        kernel,
        out_shape=[jax.ShapeDtypeStruct(shape, kind) for shape, kind in out_shape],
        in_specs=[pl.BlockSpec(memory_space=pltpu.SMEM)] + [vmem] * len(inputs),
        out_specs=[vmem] * len(out_shape),
        scratch_shapes=scratch,
        compiler_params=params(24),
        name=name,
    )(where, *inputs)


def tail_sums(where, weights, profit_pair, slots, lines):
    share, rows = weights[0].shape
    cols = profit_pair[0].shape[1]
    books = share * slots
    half = books // lines // CORES
    others = (lines // 2 - 1) * half
    wide = cols + LANES
    total = pltpu.VMEM((books, wide), F32)
    kept = [((books, CORES * rows), BF16)]
    *away, held = tail_call(
        functools.partial(away_kernel, slots, lines),
        "away_sums",
        [((others, wide), jnp.int16)] * CORES + kept,
        [total],
        where,
        [*weights, *profit_pair],
    )
    kinds = [(half, jnp.int16), (others, F32), (half, F32)]
    outs = tail_call(
        functools.partial(home_kernel, lines),
        "home_sums",
        [((n, wide), kind) for n, kind in kinds for _ in range(CORES)],
        [total],
        where,
        [held, *profit_pair],
    )
    return away, outs[0:2], outs[2:4], outs[4:6]


def relay_kernel(words_ref, plain_ref, out_ref):
    total, mass = get_words(words_ref)
    own_total, own_mass = get_plain(plain_ref)
    put_words(out_ref, total + own_total, mass + own_mass)


def relay(words, plain):
    return pl.pallas_call(
        relay_kernel,
        out_shape=jax.ShapeDtypeStruct(words.shape, jnp.int16),
        compiler_params=params(16),
        name="relay",
    )(words, plain)


def finish_kernel(where_ref, *refs):
    groups, out_ref = (refs[: len(refs) // 2], refs[len(refs) // 2 : -1]), refs[-1]
    cols = groups[0][0].shape[1] - LANES
    for side, group in enumerate(groups):
        total, mass = get_plain(group[0])
        for words_ref in group[1:]:
            more, more_mass = get_words(words_ref)
            total, mass = total + more, mass + more_mass
        core = where_ref[1] if side == 0 else 1 - where_ref[1]
        out_ref[:, pl.ds(pl.multiple_of(core * cols, cols), cols)] = total * (1.0 / mass)


def finish(where, groups):
    half, wide = groups[0][0].shape
    inputs = [*groups[0], *groups[1]]
    vmem = pl.BlockSpec(memory_space=pltpu.VMEM)
    return pl.pallas_call(
        finish_kernel,
        out_shape=jax.ShapeDtypeStruct((half, (wide - LANES) * CORES), F32),
        in_specs=[pl.BlockSpec(memory_space=pltpu.SMEM)] + [vmem] * len(inputs),
        out_specs=vmem,
        compiler_params=params(16),
        name="finish",
    )(where, *inputs)


def body(shocks, loadings, delta, gamma, kappa, book_of, bracket_low, bracket_high, rank):
    inst_cols = loadings.shape[1]
    books = bracket_low.shape[0]
    slots = lax.axis_size("inst")
    lines = lax.axis_size("scen") // CORES
    share = books // slots
    scale = (books / (inst_cols * slots)) ** 0.5
    inst = lax.axis_index("inst")
    scen = lax.axis_index("scen")
    core, line = scen % CORES, scen // CORES
    where = jnp.stack([inst, core, line]).astype(jnp.int32)

    mine, theirs, *sums = gather_and_revalue(
        where,
        shocks,
        loadings,
        delta[None, :],
        gamma[None, :],
        kappa[None, :],
        book_of[None, :],
        books,
    )
    got = swap(theirs, "scen", 1)

    most = shocks.shape[0] * lax.axis_size("scen") // RANK_PART
    own = lambda v: jnp.tile(lax.dynamic_slice_in_dim(v, inst * share, share, 0), LANES // share)[None, :]
    low, high, own_rank = own(bracket_low), own(bracket_high), own(rank)
    parts = [sums[0]] + [swap(sums[slot], "inst", slot) for slot in range(slots - 1, 0, -1)]
    value, lows = book_values(scale, most, parts)
    lists = [lows] + [swap(lows, "scen", CORES * k) for k in [*range(1, lines, 2), *range(2, lines, 2)]]
    lists = lists + [swap(v, "scen", 1) for v in lists]
    weight, row = quantiles(most, low, high, own_rank, value, lists)
    far = {slot: swap(weight, "inst", slot) for slot in range(slots - 1, 0, -1)}
    far[slots - 1], here = lax.optimization_barrier((far[slots - 1], bring(got)))
    weights = [weight] + [far[slot] for slot in range(1, slots)]
    weights = weights + [swap(w, "scen", 1) for w in weights]

    away, partner, handled, plain = tail_sums(where, weights, [mine, here], slots, lines)
    half = books // lines // CORES
    groups = []
    for side in range(CORES):
        passed = swap(away[side], "scen", CORES)
        sent = relay(passed, handled[side])
        words = []
        for k in range(1, lines // 2):
            block = sent[(k - 1) * half : k * half]
            words.append(swap(block, "scen", (CORES * (2 * k + 1)) ^ side))
        first = plain[0] if side == 0 else swap(plain[1], "scen", 1)
        groups.append([first, swap(partner[side], "scen", CORES ^ side), *words])
    return finish(where, groups), row[0, :share]


def solution(mesh):
    placed = (
        P("scen", "inst"),
        P(None, "inst"),
        P("inst"),
        P("inst"),
        P("inst"),
        P("inst"),
        P(),
        P(),
        P(),
    )
    return jax.shard_map(
        body, mesh=mesh, in_specs=placed, out_specs=(P("scen", "inst"), P("inst")), check_vma=False
    )
```

```python
import functools

import jax
import jax.numpy as jnp
from jax import lax
from jax.experimental import pallas as pl
from jax.experimental.pallas import tpu as pltpu
from jax.sharding import PartitionSpec as P

PIVOTS = 64
ROUNDS = 3
CORES = 2
LANES = 128
UPPER = 9
ROW_RUN = 256
RANK_PART = 64

tail_width = 0.5
bracket_unit = 0.125
top16 = 32600.0
octave = 0.6931471805599453
finest = 8.0
half_word = 16384.0

BF16 = jnp.bfloat16
F32 = jnp.float32


def params(megabytes):
    return pltpu.CompilerParams(vmem_limit_bytes=megabytes * 2**20)


def dot(a, b):
    return jnp.dot(a, b, preferred_element_type=F32)


def swap(value, axis, flip):
    n = lax.axis_size(axis)
    return lax.ppermute(value, axis, [(k, k ^ flip) for k in range(n)])


def tiles(width, tile):
    return [slice(at, at + tile) for at in range(0, width, tile)]


def stage_kernel(slots, near, far, where_ref, shocks_ref, book_ref, loadings_ref, first_ref, near_ref, far_ref, onehot_ref, own, sems):
    depth = shocks_ref.shape[1]
    cols, books = onehot_ref.shape
    share = books // slots
    rows_of = lambda flip: pl.ds(pl.multiple_of((where_ref[0] ^ flip) * depth, depth), depth)
    parts = tiles(cols, cols // 4)
    own_copies = [
        pltpu.make_async_copy(loadings_ref.at[rows_of(0), part], own.at[:, part], sems.at[k])
        for k, part in enumerate(parts)
    ]
    rest_copies = [
        pltpu.make_async_copy(
            loadings_ref.at[rows_of(flip), :],
            ref.at[k * depth : (k + 1) * depth, :],
            sems.at[len(parts) + flip - 1],
        )
        for ref, flips in ((near_ref, near), (far_ref, far))
        for k, flip in enumerate(flips)
    ]
    for copy in own_copies + rest_copies:
        copy.start()
    tile = cols // 8
    lane = lax.broadcasted_iota(jnp.int32, (tile, LANES), 1)
    for part in tiles(cols, tile):
        book = jnp.broadcast_to(book_ref[:, part], (LANES, tile)).T
        for at in range(0, books, LANES):
            known = (((lane + at) // share) ^ where_ref[0]) * share + (lane + at) % share
            onehot_ref[part, at : at + LANES] = jnp.where(book == known, 1.0, 0.0).astype(BF16)
    for copy, part in zip(own_copies, parts):
        copy.wait()
        first_ref[:, part] = dot(shocks_ref[...], own[:, part])
    for copy in rest_copies:
        copy.wait()


def stage(where, shocks, book_of, loadings, slots, near, far, books):
    rows, depth = shocks.shape
    cols = loadings.shape[1]
    vmem = pl.BlockSpec(memory_space=pltpu.VMEM)
    return pl.pallas_call(
        functools.partial(stage_kernel, slots, near, far),
        out_shape=[
            jax.ShapeDtypeStruct((rows, cols), F32),
            jax.ShapeDtypeStruct((len(near) * depth, cols), BF16),
            jax.ShapeDtypeStruct((len(far) * depth, cols), BF16),
            jax.ShapeDtypeStruct((cols, books), BF16),
        ],
        in_specs=[pl.BlockSpec(memory_space=pltpu.SMEM), vmem, vmem, pl.BlockSpec(memory_space=pltpu.HBM)],
        out_specs=[vmem] * 4,
        scratch_shapes=[pltpu.VMEM((depth, cols), BF16), pltpu.SemaphoreType.DMA((3 + slots,))],
        compiler_params=params(16),
        cost_estimate=pl.CostEstimate(
            flops=2 * rows * depth * cols, bytes_accessed=2 * loadings.size, transcendentals=0
        ),
        name="stage",
    )(where, shocks, book_of, loadings)


def add_moves_kernel(*refs):
    shock_refs, (rest_ref, before_ref, after_ref) = refs[:-3], refs[-3:]
    depth = shock_refs[0].shape[1]
    cols = after_ref.shape[1]
    for part in tiles(cols, cols // 8):
        total = before_ref[:, part]
        for k, shock_ref in enumerate(shock_refs):
            total = total + dot(shock_ref[...], rest_ref[k * depth : (k + 1) * depth, part])
        after_ref[:, part] = total


def add_moves(shocks, rest, before):
    vmem = pl.BlockSpec(memory_space=pltpu.VMEM)
    rows, cols = before.shape
    depth = shocks[0].shape[1]
    return pl.pallas_call(
        add_moves_kernel,
        out_shape=jax.ShapeDtypeStruct((rows, cols), F32),
        in_specs=[vmem] * (len(shocks) + 2),
        out_specs=vmem,
        input_output_aliases={len(shocks) + 1: 0},
        compiler_params=params(16),
        cost_estimate=pl.CostEstimate(
            flops=2 * rows * depth * cols * len(shocks), bytes_accessed=8 * rows * cols, transcendentals=0
        ),
        name="add_moves",
    )(*shocks, rest, before)


def profit_kernel(count, where_ref, *refs):
    top_refs, low_refs = refs[:count], refs[count : 2 * count]
    rest_ref, first_ref, delta_ref, gamma_ref, kappa_ref, onehot_ref = refs[2 * count : 2 * count + 6]
    mine_ref, theirs_ref = refs[2 * count + 6 : 2 * count + 8]
    sum_refs, (total, held, joined, sems) = refs[2 * count + 8 : -4], refs[-4:]
    upper, depth = top_refs[0].shape
    part_cols = mine_ref.shape[1]
    tile = part_cols // 4
    share = sum_refs[0].shape[0]
    for k in range(count):
        joined[k, :upper, :] = top_refs[k][...]
        joined[k, upper:, :] = low_refs[k][...]
    fresh, copies = True, []
    for side, out_ref in ((1 - where_ref[1], held), (where_ref[1], mine_ref)):
        for spot in tiles(part_cols, tile):
            part = pl.ds(pl.multiple_of(side * part_cols + spot.start, tile), tile)
            pieces = []
            for run in tiles(joined.shape[1], ROW_RUN):
                moves = first_ref[run, part]
                for k in range(count):
                    moves = moves + dot(joined[k, run, :], rest_ref[k * depth : (k + 1) * depth, part])
                value = moves * (delta_ref[:, part] + moves * (gamma_ref[:, part] + moves * kappa_ref[:, part]))
                pieces.append(value.astype(BF16))
            profit = jnp.concatenate(pieces, axis=0)
            out_ref[:, spot] = profit
            if out_ref is held:
                copies.append(pltpu.make_async_copy(held.at[:, spot], theirs_ref.at[:, spot], sems.at[len(copies)]))
                copies[-1].start()
            sums = dot(profit, onehot_ref[part, :])
            total[...] = sums if fresh else total[...] + sums
            fresh = False
    turned = total[...].T
    for slot, sum_ref in enumerate(sum_refs):
        sum_ref[...] = turned[slot * share : (slot + 1) * share, :]
    for copy in copies:
        copy.wait()


def profits(where, tops, lows, rest, first, delta, gamma, kappa, onehot, slots):
    rows, cols = first.shape
    books = onehot.shape[1]
    depth = tops[0].shape[1]
    vmem = pl.BlockSpec(memory_space=pltpu.VMEM)
    out_shape = [jax.ShapeDtypeStruct((rows, cols // CORES), BF16)] * 2
    out_shape += [jax.ShapeDtypeStruct((books // slots, rows), F32)] * slots
    return pl.pallas_call(
        functools.partial(profit_kernel, len(tops)),
        out_shape=out_shape,
        in_specs=[pl.BlockSpec(memory_space=pltpu.SMEM)] + [vmem] * (2 * len(tops) + 6),
        out_specs=[vmem, pl.BlockSpec(memory_space=pltpu.HBM)] + [vmem] * slots,
        scratch_shapes=[
            pltpu.VMEM((rows, books), F32),
            pltpu.VMEM((rows, cols // CORES), BF16),
            pltpu.VMEM((len(tops), rows, depth), BF16),
            pltpu.SemaphoreType.DMA((4,)),
        ],
        compiler_params=params(16),
        cost_estimate=pl.CostEstimate(
            flops=2 * rows * cols * (depth * len(tops) + books),
            bytes_accessed=6 * rows * cols,
            transcendentals=0,
        ),
        name="profits",
    )(where, *tops, *lows, rest, first, delta, gamma, kappa, onehot)


def gather_and_revalue(where, shocks, loadings, delta, gamma, kappa, book_of, books):
    slots = lax.axis_size("inst")
    inner = 1
    while inner * inner * 4 <= slots:
        inner *= 2
    outer = slots // inner
    upper = shocks.shape[0] // 16 * UPPER
    along = [f for f in range(1, inner)]
    across = [f * inner for f in range(1, outer)]
    corners = [(a, b) for a in along for b in across]
    near = {f: swap(shocks, "inst", f) for f in along + across}
    first, near_loads, far_loads, onehot = stage(
        where, shocks, book_of, loadings, slots, along + across, [a ^ b for a, b in corners], books
    )
    tops = [swap(near[a][:upper], "inst", b) for a, b in corners]
    lows = [swap(near[b][upper:], "inst", a) for a, b in corners]
    first = add_moves([near[f] for f in along + across], near_loads, first)
    return profits(where, tops, lows, far_loads, first, delta, gamma, kappa, onehot, slots)


def sorting_pairs(n):
    pairs, p = [], 1
    while p < n:
        k = p
        while k:
            for j in range(k % p, n - k, 2 * k):
                for i in range(j, j + min(k, n - j - k)):
                    if i // (2 * p) == (i + k) // (2 * p):
                        pairs.append((i, i + k))
            k //= 2
        p *= 2
    return pairs


def compare(values, pairs):
    for i, j in pairs:
        values[i], values[j] = jnp.minimum(values[i], values[j]), jnp.maximum(values[i], values[j])
    return values


def merged(one, other, most):
    n = len(one)
    if 2 * n <= most:
        values = one + other[::-1]
    else:
        values = [jnp.minimum(a, b) for a, b in zip(one, other[::-1])]
    n = len(values)
    stride = n // 2
    while stride:
        compare(values, [(i, i + stride) for i in range(n) if not i & stride])
        stride //= 2
    return values


def lowest(values, share, most):
    values = compare(list(values), sorting_pairs(len(values)))
    for axis, shift in [(0, 4), (0, 2), (0, 1)] + [(1, shift) for shift in doubling(share, LANES)]:
        values = merged(values, [pltpu.roll(v, shift, axis) for v in values], most)
    return values


def doubling(start, stop):
    while start < stop:
        yield start
        start *= 2


def blocks_of(ref):
    return [ref[at : at + 8, :] for at in range(0, ref.shape[0], 8)]


def book_value_kernel(scale, most, *refs):
    part_refs, (value_ref, list_ref) = refs[:-2], refs[-2:]
    value = part_refs[0][...]
    for part_ref in part_refs[1:]:
        value = value + part_ref[...]
    value = value * scale
    value_ref[...] = value
    share, rows = value.shape
    groups = LANES // share
    depth = rows // groups
    columns = jnp.concatenate([value[:, at : at + depth] for at in range(0, rows, depth)], axis=0).T
    values = lowest([columns[at : at + 8, :] for at in range(0, depth, 8)], share, most)
    place = lax.broadcasted_iota(jnp.int32, (8, LANES), 0)
    place = place + lax.broadcasted_iota(jnp.int32, (8, LANES), 1) // share * 8
    for at in range(0, most, 8 * groups):
        block = values[at]
        for k in range(1, 8 * groups):
            block = jnp.where(place == k, values[at + k], block)
        list_ref[at // groups : at // groups + 8, :] = block


def book_values(scale, most, parts):
    share, rows = parts[0].shape
    return pl.pallas_call(
        functools.partial(book_value_kernel, scale, most),
        out_shape=[
            jax.ShapeDtypeStruct((share, rows), F32),
            jax.ShapeDtypeStruct((most * share // LANES, LANES), F32),
        ],
        compiler_params=params(16),
        name="book_values",
    )(*parts)


def quantile_kernel(most, low_ref, high_ref, rank_ref, value_ref, *refs):
    list_refs, (weight_ref, quantile_ref) = refs[:-2], refs[-2:]
    share, rows = value_ref.shape
    values = lowest([block for ref in list_refs for block in blocks_of(ref)], share, most)
    rank = jnp.broadcast_to(rank_ref[...], (8, LANES))
    sought = values[0]
    for k in range(1, most):
        sought = jnp.where(rank > k, values[k], sought)
    sought = sought[:1, :]
    lower = low_ref[...].astype(F32) * bracket_unit
    upper = high_ref[...].astype(F32) * bracket_unit
    levels = lax.broadcasted_iota(jnp.int32, (PIVOTS, LANES), 0).astype(F32)
    for _ in range(ROUNDS):
        spacing = (upper - lower) / (PIVOTS - 1)
        below = jnp.where(lower + levels * spacing < sought, 1.0, 0.0)
        chosen = jnp.clip(jnp.sum(below, axis=0, keepdims=True), 1.0, float(PIVOTS - 1))
        lower, upper = lower + (chosen - 1.0) * spacing, lower + chosen * spacing
    quantile = (lower + upper) * 0.5
    quantile_ref[...] = jnp.broadcast_to(quantile, quantile_ref.shape)
    column = jnp.broadcast_to(quantile, (LANES, LANES)).T[:share, :]
    column = jnp.concatenate([column] * (rows // LANES), axis=1)
    weight_ref[...] = jax.nn.sigmoid((column - value_ref[...]) / tail_width).astype(BF16)


def quantiles(most, low, high, rank, value, lists):
    share, rows = value.shape
    return pl.pallas_call(
        functools.partial(quantile_kernel, most),
        out_shape=[
            jax.ShapeDtypeStruct((share, rows), BF16),
            jax.ShapeDtypeStruct((8, LANES), F32),
        ],
        compiler_params=params(16),
        name="quantiles",
    )(low, high, rank, value, *lists)


def encode(total, mass):
    top = jnp.maximum(jnp.max(jnp.abs(total), axis=1, keepdims=True), 1e-30)
    level = jnp.ceil(jnp.log(top * (1.0 / top16)) * (finest / octave))
    words = jnp.round(total * jnp.exp(level * (-octave / finest)))
    mass = jnp.maximum(mass, 1e-30)
    power = jnp.ceil(jnp.log(mass) * (1.0 / octave))
    scaled = mass * jnp.exp(power * -octave) * half_word
    upper = jnp.floor(scaled)
    lower = jnp.round((scaled - upper) * half_word)
    column = lax.broadcasted_iota(jnp.int32, (total.shape[0], LANES), 1)
    side = jnp.where(column == 0, level, 0.0)
    side = jnp.where(column == 1, power, side)
    side = jnp.where(column == 2, upper, side)
    side = jnp.where(column == 3, lower, side)
    return words.astype(jnp.int32).astype(jnp.int16), side.astype(jnp.int32).astype(jnp.int16)


def put_words(ref, total, mass):
    words, side = encode(total, mass)
    cols = total.shape[1]
    ref[:, :cols] = words
    ref[:, cols:] = side


def get_words(ref):
    cols = ref.shape[1] - LANES
    side = ref[:, cols:].astype(F32)
    level, power, upper, lower = (side[:, k : k + 1] for k in range(4))
    mass = (upper + lower * (1.0 / half_word)) * (1.0 / half_word) * jnp.exp(power * octave)
    total = ref[:, :cols].astype(F32) * jnp.exp(level * (octave / finest))
    return total, mass


def get_plain(ref):
    cols = ref.shape[1] - LANES
    return ref[:, :cols], ref[:, cols : cols + 1]


def sum_rows(weights, profit_refs, total, spot):
    cols = total.shape[1] - LANES
    for part in tiles(cols, cols // 4):
        result = dot(weights[0], profit_refs[0][:, part])
        for weight, profit_ref in zip(weights[1:], profit_refs[1:]):
            result = result + dot(weight, profit_ref[:, part])
        total[spot, part] = result
    put_mass(weights, total, spot)


def put_mass(weights, total, spot):
    mass = sum(jnp.sum(weight.astype(F32), axis=1, keepdims=True) for weight in weights)
    total[spot, total.shape[1] - LANES :] = jnp.broadcast_to(mass, (mass.shape[0], LANES))


def halves(where_ref, total, line, block):
    half = block // CORES
    for side in range(CORES):
        core = where_ref[1] if side == 0 else 1 - where_ref[1]
        value = total[pl.ds(pl.multiple_of(line * block + core * half, half), half), :]
        yield side, value


def arrange(slots, lines, where_ref, weight_refs, held):
    share = weight_refs[0].shape[0]
    block = share * slots // lines
    piece = min(share, block)
    away = [line for line in range(2, lines, 2)]
    order = away + [1] + [line for line in range(3, lines, 2)] + [0]
    for slot, ref in enumerate(weight_refs):
        for at in range(0, share, piece):
            start = (where_ref[0] ^ slot) * share + at
            line = start // block
            flip = where_ref[2] ^ line
            place = 0
            for k, known in enumerate(order):
                place = place + jnp.where(flip == known, k, 0)
            to = pl.multiple_of(place * block + (start - line * block), piece)
            held[pl.ds(to, piece), :] = ref[at : at + piece, :]
    return len(away) * block


def own_kernel(slots, lines, where_ref, *refs):
    weight_refs, (profit_ref, held, part_ref) = refs[:slots], refs[slots:]
    depth = arrange(slots, lines, where_ref, weight_refs, held)
    sum_rows([held[:depth, :]], [profit_ref], part_ref, slice(0, depth))


def away_kernel(slots, lines, where_ref, *refs):
    weight_refs, (part_ref, profit_ref) = refs[:slots], refs[slots : slots + 2]
    away_refs, (held, total) = refs[slots + 2 : -2], refs[-2:]
    depth = arrange(slots, lines, where_ref, weight_refs, held)
    sum_rows([held[:depth, :]], [profit_ref], total, slice(0, depth))
    total[...] += part_ref[...]
    cols = total.shape[1] - LANES
    block = held.shape[0] // lines
    half = block // CORES
    for k in range(depth // block):
        for side, value in halves(where_ref, total, k, block):
            put_words(away_refs[side].at[k * half : (k + 1) * half, :], value[:, :cols], value[:, cols : cols + 1])


def home_kernel(lines, where_ref, *refs):
    helds, profit_refs = refs[:CORES], refs[CORES : 2 * CORES]
    partner_refs, handled_refs, own_refs = (refs[k : k + 2] for k in range(2 * CORES, 2 * CORES + 6, 2))
    total = refs[-1]
    block = helds[0].shape[0] // lines
    half = block // CORES
    cols = total.shape[1] - LANES
    skip = lines // 2 - 1
    spot = slice(skip * block, lines * block)
    sum_rows([held[spot, :] for held in helds], profit_refs, total, spot)
    for side, value in halves(where_ref, total, skip, block):
        put_words(partner_refs[side], value[:, :cols], value[:, cols : cols + 1])
    for k in range(skip):
        for side, value in halves(where_ref, total, skip + 1 + k, block):
            handled_refs[side][k * half : (k + 1) * half, :] = value
    for side, value in halves(where_ref, total, lines - 1, block):
        own_refs[side][...] = value


def bring_kernel(far_ref, near_ref, sem):
    copy = pltpu.make_async_copy(far_ref, near_ref, sem)
    copy.start()
    copy.wait()


def bring(far):
    return pl.pallas_call(
        bring_kernel,
        out_shape=jax.ShapeDtypeStruct(far.shape, far.dtype),
        in_specs=[pl.BlockSpec(memory_space=pltpu.HBM)],
        out_specs=pl.BlockSpec(memory_space=pltpu.VMEM),
        scratch_shapes=[pltpu.SemaphoreType.DMA],
        compiler_params=params(16),
        cost_estimate=pl.CostEstimate(flops=0, bytes_accessed=8 * far.size, transcendentals=0),
        name="bring",
    )(far)


def tail_call(kernel, name, out_shape, scratch, where, inputs):
    vmem = pl.BlockSpec(memory_space=pltpu.VMEM)
    return pl.pallas_call(
        kernel,
        out_shape=[jax.ShapeDtypeStruct(shape, kind) for shape, kind in out_shape],
        in_specs=[pl.BlockSpec(memory_space=pltpu.SMEM)] + [vmem] * len(inputs),
        out_specs=[vmem] * len(out_shape),
        scratch_shapes=scratch,
        compiler_params=params(24),
        cost_estimate=pl.CostEstimate(
            flops=0, bytes_accessed=4 * sum(v.size * v.dtype.itemsize for v in inputs), transcendentals=0
        ),
        name=name,
    )(where, *inputs)


def tail_sums(where, weights, others, profit_pair, slots, lines):
    share, rows = weights[0].shape
    cols = profit_pair[0].shape[1]
    books = share * slots
    half = books // lines // CORES
    away_rows = (lines // 2 - 1) * half
    wide = cols + LANES
    held = ((books, rows), BF16)
    part_shape = (away_rows * CORES, wide)
    first, part = tail_call(
        functools.partial(own_kernel, slots, lines),
        "own_sums",
        [held, (part_shape, F32)],
        [],
        where,
        [*weights, profit_pair[0]],
    )
    *away, second = tail_call(
        functools.partial(away_kernel, slots, lines),
        "away_sums",
        [((away_rows, wide), jnp.int16)] * CORES + [held],
        [pltpu.VMEM(part_shape, F32)],
        where,
        [*others, part, profit_pair[1]],
    )
    kinds = [(half, jnp.int16), (away_rows, F32), (half, F32)]
    outs = tail_call(
        functools.partial(home_kernel, lines),
        "home_sums",
        [((n, wide), kind) for n, kind in kinds for _ in range(CORES)],
        [pltpu.VMEM((books, wide), F32)],
        where,
        [first, second, *profit_pair],
    )
    return away, outs[0:2], outs[2:4], outs[4:6]


def relay_kernel(words_ref, plain_ref, out_ref):
    total, mass = get_words(words_ref)
    own_total, own_mass = get_plain(plain_ref)
    put_words(out_ref, total + own_total, mass + own_mass)


def relay(words, plain):
    return pl.pallas_call(
        relay_kernel,
        out_shape=jax.ShapeDtypeStruct(words.shape, jnp.int16),
        compiler_params=params(16),
        name="relay",
    )(words, plain)


def finish_kernel(where_ref, *refs):
    groups, out_ref = (refs[: len(refs) // 2], refs[len(refs) // 2 : -1]), refs[-1]
    cols = groups[0][0].shape[1] - LANES
    for side, group in enumerate(groups):
        total, mass = get_plain(group[0])
        for words_ref in group[1:]:
            more, more_mass = get_words(words_ref)
            total, mass = total + more, mass + more_mass
        core = where_ref[1] if side == 0 else 1 - where_ref[1]
        out_ref[:, pl.ds(pl.multiple_of(core * cols, cols), cols)] = total * (1.0 / mass)


def finish(where, groups):
    half, wide = groups[0][0].shape
    inputs = [*groups[0], *groups[1]]
    vmem = pl.BlockSpec(memory_space=pltpu.VMEM)
    return pl.pallas_call(
        finish_kernel,
        out_shape=jax.ShapeDtypeStruct((half, (wide - LANES) * CORES), F32),
        in_specs=[pl.BlockSpec(memory_space=pltpu.SMEM)] + [vmem] * len(inputs),
        out_specs=vmem,
        compiler_params=params(16),
        name="finish",
    )(where, *inputs)


def body(shocks, loadings, delta, gamma, kappa, book_of, bracket_low, bracket_high, rank):
    inst_cols = loadings.shape[1]
    books = bracket_low.shape[0]
    slots = lax.axis_size("inst")
    lines = lax.axis_size("scen") // CORES
    share = books // slots
    scale = (books / (inst_cols * slots)) ** 0.5
    inst = lax.axis_index("inst")
    scen = lax.axis_index("scen")
    core, line = scen % CORES, scen // CORES
    where = jnp.stack([inst, core, line]).astype(jnp.int32)

    mine, theirs, *sums = gather_and_revalue(
        where,
        shocks,
        loadings,
        delta[None, :],
        gamma[None, :],
        kappa[None, :],
        book_of[None, :],
        books,
    )
    got = swap(theirs, "scen", 1)

    most = shocks.shape[0] * lax.axis_size("scen") // RANK_PART
    own = lambda v: jnp.tile(lax.dynamic_slice_in_dim(v, inst * share, share, 0), LANES // share)[None, :]
    low, high, own_rank = own(bracket_low), own(bracket_high), own(rank)
    parts = [sums[0]] + [swap(sums[slot], "inst", slot) for slot in range(slots - 1, 0, -1)]
    value, lows = book_values(scale, most, parts)
    lists = [lows] + [swap(lows, "scen", CORES * k) for k in [*range(1, lines, 2), *range(2, lines, 2)]]
    lists = lists + [swap(v, "scen", 1) for v in lists]
    weight, row = quantiles(most, low, high, own_rank, value, lists)
    far = {slot: swap(weight, "inst", slot) for slot in range(slots - 1, 0, -1)}
    far[slots - 1], here = lax.optimization_barrier((far[slots - 1], bring(got)))
    weights = [weight] + [far[slot] for slot in range(1, slots)]
    others = [swap(w, "scen", 1) for w in weights]

    away, partner, handled, plain = tail_sums(where, weights, others, [mine, here], slots, lines)
    half = books // lines // CORES
    groups = []
    for side in range(CORES):
        passed = swap(away[side], "scen", CORES)
        sent = relay(passed, handled[side])
        words = []
        for k in range(1, lines // 2):
            block = sent[(k - 1) * half : k * half]
            words.append(swap(block, "scen", (CORES * (2 * k + 1)) ^ side))
        first = plain[0] if side == 0 else swap(plain[1], "scen", 1)
        groups.append([first, swap(partner[side], "scen", CORES ^ side), *words])
    return finish(where, groups), row[0, :share]


def solution(mesh):
    placed = (
        P("scen", "inst"),
        P(None, "inst"),
        P("inst"),
        P("inst"),
        P("inst"),
        P("inst"),
        P(),
        P(),
        P(),
    )
    return jax.shard_map(
        body, mesh=mesh, in_specs=placed, out_specs=(P("scen", "inst"), P("inst")), check_vma=False
    )
```

```python
import functools

import jax
import jax.numpy as jnp
from jax import lax
from jax.experimental import pallas as pl
from jax.experimental.pallas import tpu as pltpu
from jax.sharding import PartitionSpec as P

PIVOTS = 64
ROUNDS = 3
CORES = 2
LANES = 128
UPPER = 9
ROW_RUN = 256
RANK_PART = 64

tail_width = 0.5
bracket_unit = 0.125
top16 = 32600.0
octave = 0.6931471805599453
finest = 8.0
half_word = 16384.0

BF16 = jnp.bfloat16
F32 = jnp.float32


def params(megabytes):
    return pltpu.CompilerParams(vmem_limit_bytes=megabytes * 2**20)


def dot(a, b):
    return jnp.dot(a, b, preferred_element_type=F32)


def swap(value, axis, flip):
    n = lax.axis_size(axis)
    return lax.ppermute(value, axis, [(k, k ^ flip) for k in range(n)])


def tiles(width, tile):
    return [slice(at, at + tile) for at in range(0, width, tile)]


def stage_kernel(slots, near, far, where_ref, shocks_ref, book_ref, loadings_ref, first_ref, near_ref, far_ref, onehot_ref, own, sems):
    depth = shocks_ref.shape[1]
    cols, books = onehot_ref.shape
    share = books // slots
    rows_of = lambda flip: pl.ds(pl.multiple_of((where_ref[0] ^ flip) * depth, depth), depth)
    parts = tiles(cols, cols // 4)
    own_copies = [
        pltpu.make_async_copy(loadings_ref.at[rows_of(0), part], own.at[:, part], sems.at[k])
        for k, part in enumerate(parts)
    ]
    rest_copies = [
        pltpu.make_async_copy(
            loadings_ref.at[rows_of(flip), :],
            ref.at[k * depth : (k + 1) * depth, :],
            sems.at[len(parts) + flip - 1],
        )
        for ref, flips in ((near_ref, near), (far_ref, far))
        for k, flip in enumerate(flips)
    ]
    for copy in own_copies + rest_copies:
        copy.start()
    tile = cols // 8
    lane = lax.broadcasted_iota(jnp.int32, (tile, LANES), 1)
    for part in tiles(cols, tile):
        book = jnp.broadcast_to(book_ref[:, part], (LANES, tile)).T
        for at in range(0, books, LANES):
            known = (((lane + at) // share) ^ where_ref[0]) * share + (lane + at) % share
            onehot_ref[part, at : at + LANES] = jnp.where(book == known, 1.0, 0.0).astype(BF16)
    for copy, part in zip(own_copies, parts):
        copy.wait()
        first_ref[:, part] = dot(shocks_ref[...], own[:, part])
    for copy in rest_copies:
        copy.wait()


def stage(where, shocks, book_of, loadings, slots, near, far, books):
    rows, depth = shocks.shape
    cols = loadings.shape[1]
    vmem = pl.BlockSpec(memory_space=pltpu.VMEM)
    return pl.pallas_call(
        functools.partial(stage_kernel, slots, near, far),
        out_shape=[
            jax.ShapeDtypeStruct((rows, cols), F32),
            jax.ShapeDtypeStruct((len(near) * depth, cols), BF16),
            jax.ShapeDtypeStruct((len(far) * depth, cols), BF16),
            jax.ShapeDtypeStruct((cols, books), BF16),
        ],
        in_specs=[pl.BlockSpec(memory_space=pltpu.SMEM), vmem, vmem, pl.BlockSpec(memory_space=pltpu.HBM)],
        out_specs=[vmem] * 4,
        scratch_shapes=[pltpu.VMEM((depth, cols), BF16), pltpu.SemaphoreType.DMA((3 + slots,))],
        compiler_params=params(16),
        cost_estimate=pl.CostEstimate(
            flops=2 * rows * depth * cols, bytes_accessed=2 * loadings.size, transcendentals=0
        ),
        name="stage",
    )(where, shocks, book_of, loadings)


def add_moves_kernel(*refs):
    shock_refs, (rest_ref, before_ref, after_ref) = refs[:-3], refs[-3:]
    depth = shock_refs[0].shape[1]
    cols = after_ref.shape[1]
    for part in tiles(cols, cols // 8):
        total = before_ref[:, part]
        for k, shock_ref in enumerate(shock_refs):
            total = total + dot(shock_ref[...], rest_ref[k * depth : (k + 1) * depth, part])
        after_ref[:, part] = total


def add_moves(shocks, rest, before):
    vmem = pl.BlockSpec(memory_space=pltpu.VMEM)
    rows, cols = before.shape
    depth = shocks[0].shape[1]
    return pl.pallas_call(
        add_moves_kernel,
        out_shape=jax.ShapeDtypeStruct((rows, cols), F32),
        in_specs=[vmem] * (len(shocks) + 2),
        out_specs=vmem,
        input_output_aliases={len(shocks) + 1: 0},
        compiler_params=params(16),
        cost_estimate=pl.CostEstimate(
            flops=2 * rows * depth * cols * len(shocks), bytes_accessed=8 * rows * cols, transcendentals=0
        ),
        name="add_moves",
    )(*shocks, rest, before)


def profit_kernel(count, where_ref, *refs):
    top_refs, low_refs = refs[:count], refs[count : 2 * count]
    rest_ref, first_ref, delta_ref, gamma_ref, kappa_ref, onehot_ref = refs[2 * count : 2 * count + 6]
    mine_ref, theirs_ref = refs[2 * count + 6 : 2 * count + 8]
    sum_refs, (total, held, joined, sems) = refs[2 * count + 8 : -4], refs[-4:]
    upper, depth = top_refs[0].shape
    part_cols = mine_ref.shape[1]
    tile = part_cols // 4
    share = sum_refs[0].shape[0]
    for k in range(count):
        joined[k, :upper, :] = top_refs[k][...]
        joined[k, upper:, :] = low_refs[k][...]
    fresh, copies = True, []
    for side, out_ref in ((1 - where_ref[1], held), (where_ref[1], mine_ref)):
        for spot in tiles(part_cols, tile):
            part = pl.ds(pl.multiple_of(side * part_cols + spot.start, tile), tile)
            pieces = []
            for run in tiles(joined.shape[1], ROW_RUN):
                moves = first_ref[run, part]
                for k in range(count):
                    moves = moves + dot(joined[k, run, :], rest_ref[k * depth : (k + 1) * depth, part])
                value = moves * (delta_ref[:, part] + moves * (gamma_ref[:, part] + moves * kappa_ref[:, part]))
                pieces.append(value.astype(BF16))
            profit = jnp.concatenate(pieces, axis=0)
            out_ref[:, spot] = profit
            if out_ref is held:
                copies.append(pltpu.make_async_copy(held.at[:, spot], theirs_ref.at[:, spot], sems.at[len(copies)]))
                copies[-1].start()
            sums = dot(profit, onehot_ref[part, :])
            total[...] = sums if fresh else total[...] + sums
            fresh = False
    turned = total[...].T
    for slot, sum_ref in enumerate(sum_refs):
        sum_ref[...] = turned[slot * share : (slot + 1) * share, :]
    for copy in copies:
        copy.wait()


def profits(where, tops, lows, rest, first, delta, gamma, kappa, onehot, slots):
    rows, cols = first.shape
    books = onehot.shape[1]
    depth = tops[0].shape[1]
    vmem = pl.BlockSpec(memory_space=pltpu.VMEM)
    out_shape = [jax.ShapeDtypeStruct((rows, cols // CORES), BF16)] * 2
    out_shape += [jax.ShapeDtypeStruct((books // slots, rows), F32)] * slots
    return pl.pallas_call(
        functools.partial(profit_kernel, len(tops)),
        out_shape=out_shape,
        in_specs=[pl.BlockSpec(memory_space=pltpu.SMEM)] + [vmem] * (2 * len(tops) + 6),
        out_specs=[vmem, pl.BlockSpec(memory_space=pltpu.HBM)] + [vmem] * slots,
        scratch_shapes=[
            pltpu.VMEM((rows, books), F32),
            pltpu.VMEM((rows, cols // CORES), BF16),
            pltpu.VMEM((len(tops), rows, depth), BF16),
            pltpu.SemaphoreType.DMA((4,)),
        ],
        compiler_params=params(16),
        cost_estimate=pl.CostEstimate(
            flops=2 * rows * cols * (depth * len(tops) + books),
            bytes_accessed=6 * rows * cols,
            transcendentals=0,
        ),
        name="profits",
    )(where, *tops, *lows, rest, first, delta, gamma, kappa, onehot)


def gather_and_revalue(where, shocks, loadings, delta, gamma, kappa, book_of, books):
    slots = lax.axis_size("inst")
    inner = 1
    while inner * inner * 4 <= slots:
        inner *= 2
    outer = slots // inner
    upper = shocks.shape[0] // 16 * UPPER
    along = [f for f in range(1, inner)]
    across = [f * inner for f in range(1, outer)]
    corners = [(a, b) for a in along for b in across]
    near = {f: swap(shocks, "inst", f) for f in along + across}
    first, near_loads, far_loads, onehot = stage(
        where, shocks, book_of, loadings, slots, along + across, [a ^ b for a, b in corners], books
    )
    tops = [swap(near[a][:upper], "inst", b) for a, b in corners]
    lows = [swap(near[b][upper:], "inst", a) for a, b in corners]
    first = add_moves([near[f] for f in along + across], near_loads, first)
    return profits(where, tops, lows, far_loads, first, delta, gamma, kappa, onehot, slots)


def sorting_pairs(n):
    pairs, p = [], 1
    while p < n:
        k = p
        while k:
            for j in range(k % p, n - k, 2 * k):
                for i in range(j, j + min(k, n - j - k)):
                    if i // (2 * p) == (i + k) // (2 * p):
                        pairs.append((i, i + k))
            k //= 2
        p *= 2
    return pairs


def compare(values, pairs):
    for i, j in pairs:
        values[i], values[j] = jnp.minimum(values[i], values[j]), jnp.maximum(values[i], values[j])
    return values


def merged(one, other, most):
    n = len(one)
    if 2 * n <= most:
        values = one + other[::-1]
    else:
        values = [jnp.minimum(a, b) for a, b in zip(one, other[::-1])]
    n = len(values)
    stride = n // 2
    while stride:
        compare(values, [(i, i + stride) for i in range(n) if not i & stride])
        stride //= 2
    return values


def lowest(values, share, most):
    values = compare(list(values), sorting_pairs(len(values)))
    for axis, shift in [(0, 4), (0, 2), (0, 1)] + [(1, shift) for shift in doubling(share, LANES)]:
        values = merged(values, [pltpu.roll(v, shift, axis) for v in values], most)
    return values


def doubling(start, stop):
    while start < stop:
        yield start
        start *= 2


def blocks_of(ref):
    return [ref[at : at + 8, :] for at in range(0, ref.shape[0], 8)]


def book_value_kernel(scale, most, *refs):
    part_refs, (value_ref, list_ref) = refs[:-2], refs[-2:]
    value = part_refs[0][...]
    for part_ref in part_refs[1:]:
        value = value + part_ref[...]
    value = value * scale
    value_ref[...] = value
    share, rows = value.shape
    groups = LANES // share
    depth = rows // groups
    columns = jnp.concatenate([value[:, at : at + depth] for at in range(0, rows, depth)], axis=0).T
    values = lowest([columns[at : at + 8, :] for at in range(0, depth, 8)], share, most)
    place = lax.broadcasted_iota(jnp.int32, (8, LANES), 0)
    place = place + lax.broadcasted_iota(jnp.int32, (8, LANES), 1) // share * 8
    for at in range(0, most, 8 * groups):
        block = values[at]
        for k in range(1, 8 * groups):
            block = jnp.where(place == k, values[at + k], block)
        list_ref[at // groups : at // groups + 8, :] = block


def book_values(scale, most, parts):
    share, rows = parts[0].shape
    return pl.pallas_call(
        functools.partial(book_value_kernel, scale, most),
        out_shape=[
            jax.ShapeDtypeStruct((share, rows), F32),
            jax.ShapeDtypeStruct((most * share // LANES, LANES), F32),
        ],
        compiler_params=params(16),
        name="book_values",
    )(*parts)


def quantile_kernel(most, low_ref, high_ref, rank_ref, value_ref, *refs):
    list_refs, (weight_ref, quantile_ref) = refs[:-2], refs[-2:]
    share, rows = value_ref.shape
    values = lowest([block for ref in list_refs for block in blocks_of(ref)], share, most)
    rank = jnp.broadcast_to(rank_ref[...], (8, LANES))
    sought = values[0]
    for k in range(1, most):
        sought = jnp.where(rank > k, values[k], sought)
    sought = sought[:1, :]
    lower = low_ref[...].astype(F32) * bracket_unit
    upper = high_ref[...].astype(F32) * bracket_unit
    levels = lax.broadcasted_iota(jnp.int32, (PIVOTS, LANES), 0).astype(F32)
    for _ in range(ROUNDS):
        spacing = (upper - lower) / (PIVOTS - 1)
        below = jnp.where(lower + levels * spacing < sought, 1.0, 0.0)
        chosen = jnp.clip(jnp.sum(below, axis=0, keepdims=True), 1.0, float(PIVOTS - 1))
        lower, upper = lower + (chosen - 1.0) * spacing, lower + chosen * spacing
    quantile = (lower + upper) * 0.5
    quantile_ref[...] = jnp.broadcast_to(quantile, quantile_ref.shape)
    column = jnp.broadcast_to(quantile, (LANES, LANES)).T[:share, :]
    column = jnp.concatenate([column] * (rows // LANES), axis=1)
    weight_ref[...] = jax.nn.sigmoid((column - value_ref[...]) / tail_width).astype(BF16)


def quantiles(most, low, high, rank, value, lists):
    share, rows = value.shape
    return pl.pallas_call(
        functools.partial(quantile_kernel, most),
        out_shape=[
            jax.ShapeDtypeStruct((share, rows), BF16),
            jax.ShapeDtypeStruct((8, LANES), F32),
        ],
        compiler_params=params(16),
        name="quantiles",
    )(low, high, rank, value, *lists)


def encode(total, mass):
    top = jnp.maximum(jnp.max(jnp.abs(total), axis=1, keepdims=True), 1e-30)
    level = jnp.ceil(jnp.log(top * (1.0 / top16)) * (finest / octave))
    words = jnp.round(total * jnp.exp(level * (-octave / finest)))
    mass = jnp.maximum(mass, 1e-30)
    power = jnp.ceil(jnp.log(mass) * (1.0 / octave))
    scaled = mass * jnp.exp(power * -octave) * half_word
    upper = jnp.floor(scaled)
    lower = jnp.round((scaled - upper) * half_word)
    column = lax.broadcasted_iota(jnp.int32, (total.shape[0], LANES), 1)
    side = jnp.where(column == 0, level, 0.0)
    side = jnp.where(column == 1, power, side)
    side = jnp.where(column == 2, upper, side)
    side = jnp.where(column == 3, lower, side)
    return words.astype(jnp.int32).astype(jnp.int16), side.astype(jnp.int32).astype(jnp.int16)


def put_words(ref, total, mass):
    words, side = encode(total, mass)
    cols = total.shape[1]
    ref[:, :cols] = words
    ref[:, cols:] = side


def get_words(ref):
    cols = ref.shape[1] - LANES
    side = ref[:, cols:].astype(F32)
    level, power, upper, lower = (side[:, k : k + 1] for k in range(4))
    mass = (upper + lower * (1.0 / half_word)) * (1.0 / half_word) * jnp.exp(power * octave)
    total = ref[:, :cols].astype(F32) * jnp.exp(level * (octave / finest))
    return total, mass


def get_plain(ref):
    cols = ref.shape[1] - LANES
    return ref[:, :cols], ref[:, cols : cols + 1]


def sum_rows(weights, profit_refs, total, spot):
    cols = total.shape[1] - LANES
    for part in tiles(cols, cols // 4):
        result = dot(weights[0], profit_refs[0][:, part])
        for weight, profit_ref in zip(weights[1:], profit_refs[1:]):
            result = result + dot(weight, profit_ref[:, part])
        total[spot, part] = result
    put_mass(weights, total, spot)


def put_mass(weights, total, spot):
    mass = sum(jnp.sum(weight.astype(F32), axis=1, keepdims=True) for weight in weights)
    total[spot, total.shape[1] - LANES :] = jnp.broadcast_to(mass, (mass.shape[0], LANES))


def halves(where_ref, total, line, block):
    half = block // CORES
    for side in range(CORES):
        core = where_ref[1] if side == 0 else 1 - where_ref[1]
        value = total[pl.ds(pl.multiple_of(line * block + core * half, half), half), :]
        yield side, value


def arrange(slots, lines, where_ref, weight_refs, held):
    share = weight_refs[0].shape[0]
    block = share * slots // lines
    piece = min(share, block)
    away = [line for line in range(2, lines, 2)]
    order = away + [1] + [line for line in range(3, lines, 2)] + [0]
    for slot, ref in enumerate(weight_refs):
        for at in range(0, share, piece):
            start = (where_ref[0] ^ slot) * share + at
            line = start // block
            flip = where_ref[2] ^ line
            place = 0
            for k, known in enumerate(order):
                place = place + jnp.where(flip == known, k, 0)
            to = pl.multiple_of(place * block + (start - line * block), piece)
            held[pl.ds(to, piece), :] = ref[at : at + piece, :]
    return len(away) * block


def own_kernel(slots, lines, where_ref, *refs):
    weight_refs, (profit_ref, held, part_ref) = refs[:slots], refs[slots:]
    depth = arrange(slots, lines, where_ref, weight_refs, held)
    sum_rows([held[:depth, :]], [profit_ref], part_ref, slice(0, depth))


def away_kernel(slots, lines, where_ref, *refs):
    weight_refs, (part_ref, profit_ref) = refs[:slots], refs[slots : slots + 2]
    away_refs, (held, total) = refs[slots + 2 : -2], refs[-2:]
    depth = arrange(slots, lines, where_ref, weight_refs, held)
    sum_rows([held[:depth, :]], [profit_ref], total, slice(0, depth))
    total[...] += part_ref[...]
    cols = total.shape[1] - LANES
    block = held.shape[0] // lines
    half = block // CORES
    for k in range(depth // block):
        for side, value in halves(where_ref, total, k, block):
            put_words(away_refs[side].at[k * half : (k + 1) * half, :], value[:, :cols], value[:, cols : cols + 1])


def home_kernel(lines, where_ref, *refs):
    helds, profit_refs = refs[:CORES], refs[CORES : 2 * CORES]
    partner_refs, handled_refs, own_refs = (refs[k : k + 2] for k in range(2 * CORES, 2 * CORES + 6, 2))
    total = refs[-1]
    block = helds[0].shape[0] // lines
    half = block // CORES
    cols = total.shape[1] - LANES
    skip = lines // 2 - 1
    spot = slice(skip * block, lines * block)
    sum_rows([held[spot, :] for held in helds], profit_refs, total, spot)
    for side, value in halves(where_ref, total, skip, block):
        put_words(partner_refs[side], value[:, :cols], value[:, cols : cols + 1])
    for k in range(skip):
        for side, value in halves(where_ref, total, skip + 1 + k, block):
            handled_refs[side][k * half : (k + 1) * half, :] = value
    for side, value in halves(where_ref, total, lines - 1, block):
        own_refs[side][...] = value


def bring_kernel(far_ref, near_ref, sem):
    copy = pltpu.make_async_copy(far_ref, near_ref, sem)
    copy.start()
    copy.wait()


def bring(far):
    return pl.pallas_call(
        bring_kernel,
        out_shape=jax.ShapeDtypeStruct(far.shape, far.dtype),
        in_specs=[pl.BlockSpec(memory_space=pltpu.HBM)],
        out_specs=pl.BlockSpec(memory_space=pltpu.VMEM),
        scratch_shapes=[pltpu.SemaphoreType.DMA],
        compiler_params=params(16),
        cost_estimate=pl.CostEstimate(flops=0, bytes_accessed=8 * far.size, transcendentals=0),
        name="bring",
    )(far)


def tail_call(kernel, name, out_shape, scratch, where, inputs):
    vmem = pl.BlockSpec(memory_space=pltpu.VMEM)
    return pl.pallas_call(
        kernel,
        out_shape=[jax.ShapeDtypeStruct(shape, kind) for shape, kind in out_shape],
        in_specs=[pl.BlockSpec(memory_space=pltpu.SMEM)] + [vmem] * len(inputs),
        out_specs=[vmem] * len(out_shape),
        scratch_shapes=scratch,
        compiler_params=params(24),
        cost_estimate=pl.CostEstimate(
            flops=0, bytes_accessed=4 * sum(v.size * v.dtype.itemsize for v in inputs), transcendentals=0
        ),
        name=name,
    )(where, *inputs)


def tail_sums(where, weights, others, profit_pair, slots, lines):
    share, rows = weights[0].shape
    cols = profit_pair[0].shape[1]
    books = share * slots
    half = books // lines // CORES
    away_rows = (lines // 2 - 1) * half
    wide = cols + LANES
    held = ((books, rows), BF16)
    part_shape = (away_rows * CORES, wide)
    first, part = tail_call(
        functools.partial(own_kernel, slots, lines),
        "own_sums",
        [held, (part_shape, F32)],
        [],
        where,
        [*weights, profit_pair[0]],
    )
    *away, second = tail_call(
        functools.partial(away_kernel, slots, lines),
        "away_sums",
        [((away_rows, wide), jnp.int16)] * CORES + [held],
        [pltpu.VMEM(part_shape, F32)],
        where,
        [*others, part, profit_pair[1]],
    )
    kinds = [(half, jnp.int16), (away_rows, F32), (half, F32)]
    outs = tail_call(
        functools.partial(home_kernel, lines),
        "home_sums",
        [((n, wide), kind) for n, kind in kinds for _ in range(CORES)],
        [pltpu.VMEM((books, wide), F32)],
        where,
        [first, second, *profit_pair],
    )
    return away, outs[0:2], outs[2:4], outs[4:6]


def relay_kernel(words_ref, plain_ref, out_ref):
    total, mass = get_words(words_ref)
    own_total, own_mass = get_plain(plain_ref)
    put_words(out_ref, total + own_total, mass + own_mass)


def relay(words, plain):
    return pl.pallas_call(
        relay_kernel,
        out_shape=jax.ShapeDtypeStruct(words.shape, jnp.int16),
        compiler_params=params(16),
        name="relay",
    )(words, plain)


def finish_kernel(where_ref, *refs):
    groups, out_ref = (refs[: len(refs) // 2], refs[len(refs) // 2 : -1]), refs[-1]
    cols = groups[0][0].shape[1] - LANES
    for side, group in enumerate(groups):
        total, mass = get_plain(group[0])
        for words_ref in group[1:]:
            more, more_mass = get_words(words_ref)
            total, mass = total + more, mass + more_mass
        core = where_ref[1] if side == 0 else 1 - where_ref[1]
        out_ref[:, pl.ds(pl.multiple_of(core * cols, cols), cols)] = total * (1.0 / mass)


def finish(where, groups):
    half, wide = groups[0][0].shape
    inputs = [*groups[0], *groups[1]]
    vmem = pl.BlockSpec(memory_space=pltpu.VMEM)
    return pl.pallas_call(
        finish_kernel,
        out_shape=jax.ShapeDtypeStruct((half, (wide - LANES) * CORES), F32),
        in_specs=[pl.BlockSpec(memory_space=pltpu.SMEM)] + [vmem] * len(inputs),
        out_specs=vmem,
        compiler_params=params(16),
        name="finish",
    )(where, *inputs)


def body(shocks, loadings, delta, gamma, kappa, book_of, bracket_low, bracket_high, rank):
    inst_cols = loadings.shape[1]
    books = bracket_low.shape[0]
    slots = lax.axis_size("inst")
    lines = lax.axis_size("scen") // CORES
    share = books // slots
    scale = (books / (inst_cols * slots)) ** 0.5
    inst = lax.axis_index("inst")
    scen = lax.axis_index("scen")
    core, line = scen % CORES, scen // CORES
    where = jnp.stack([inst, core, line]).astype(jnp.int32)

    mine, theirs, *sums = gather_and_revalue(
        where,
        shocks,
        loadings,
        delta[None, :],
        gamma[None, :],
        kappa[None, :],
        book_of[None, :],
        books,
    )

    most = shocks.shape[0] * lax.axis_size("scen") // RANK_PART
    own = lambda v: jnp.tile(lax.dynamic_slice_in_dim(v, inst * share, share, 0), LANES // share)[None, :]
    low, high, own_rank = own(bracket_low), own(bracket_high), own(rank)
    parts = [sums[0]] + [swap(sums[slot], "inst", slot) for slot in range(slots - 1, 0, -1)]
    value, lows = book_values(scale, most, parts)
    lows, theirs = lax.optimization_barrier((lows, theirs))
    got = swap(theirs, "scen", 1)
    lists = [lows] + [swap(lows, "scen", CORES * k) for k in [*range(1, lines, 2), *range(2, lines, 2)]]
    lists = lists + [swap(v, "scen", 1) for v in lists]
    weight, row = quantiles(most, low, high, own_rank, value, lists)
    far = {slot: swap(weight, "inst", slot) for slot in range(slots - 1, 0, -1)}
    far[slots - 1], here = lax.optimization_barrier((far[slots - 1], bring(got)))
    weights = [weight] + [far[slot] for slot in range(1, slots)]
    others = [swap(w, "scen", 1) for w in weights]

    away, partner, handled, plain = tail_sums(where, weights, others, [mine, here], slots, lines)
    half = books // lines // CORES
    groups = []
    for side in range(CORES):
        passed = swap(away[side], "scen", CORES)
        sent = relay(passed, handled[side])
        words = []
        for k in range(1, lines // 2):
            block = sent[(k - 1) * half : k * half]
            words.append(swap(block, "scen", (CORES * (2 * k + 1)) ^ side))
        first = plain[0] if side == 0 else swap(plain[1], "scen", 1)
        groups.append([first, swap(partner[side], "scen", CORES ^ side), *words])
    return finish(where, groups), row[0, :share]


def solution(mesh):
    placed = (
        P("scen", "inst"),
        P(None, "inst"),
        P("inst"),
        P("inst"),
        P("inst"),
        P("inst"),
        P(),
        P(),
        P(),
    )
    return jax.shard_map(
        body, mesh=mesh, in_specs=placed, out_specs=(P("scen", "inst"), P("inst")), check_vma=False
    )
```

```python
import functools

import jax
import jax.numpy as jnp
from jax import lax
from jax.experimental import pallas as pl
from jax.experimental.pallas import tpu as pltpu
from jax.sharding import PartitionSpec as P

PIVOTS = 64
ROUNDS = 3
CORES = 2
LANES = 128
UPPER = 9
ROW_RUN = 256
RANK_PART = 64

tail_width = 0.5
bracket_unit = 0.125
top16 = 32600.0
octave = 0.6931471805599453
finest = 8.0
half_word = 16384.0

BF16 = jnp.bfloat16
F32 = jnp.float32


def params(megabytes):
    return pltpu.CompilerParams(vmem_limit_bytes=megabytes * 2**20)


def dot(a, b):
    return jnp.dot(a, b, preferred_element_type=F32)


def swap(value, axis, flip):
    n = lax.axis_size(axis)
    return lax.ppermute(value, axis, [(k, k ^ flip) for k in range(n)])


def tiles(width, tile):
    return [slice(at, at + tile) for at in range(0, width, tile)]


def stage_kernel(slots, near, far, where_ref, shocks_ref, book_ref, loadings_ref, first_ref, near_ref, far_ref, onehot_ref, own, sems):
    depth = shocks_ref.shape[1]
    cols, books = onehot_ref.shape
    share = books // slots
    rows_of = lambda flip: pl.ds(pl.multiple_of((where_ref[0] ^ flip) * depth, depth), depth)
    parts = tiles(cols, cols // 4)
    own_copies = [
        pltpu.make_async_copy(loadings_ref.at[rows_of(0), part], own.at[:, part], sems.at[k])
        for k, part in enumerate(parts)
    ]
    rest_copies = [
        pltpu.make_async_copy(
            loadings_ref.at[rows_of(flip), :],
            ref.at[k * depth : (k + 1) * depth, :],
            sems.at[len(parts) + flip - 1],
        )
        for ref, flips in ((near_ref, near), (far_ref, far))
        for k, flip in enumerate(flips)
    ]
    for copy in own_copies + rest_copies:
        copy.start()
    tile = cols // 8
    lane = lax.broadcasted_iota(jnp.int32, (tile, LANES), 1)
    for part in tiles(cols, tile):
        book = jnp.broadcast_to(book_ref[:, part], (LANES, tile)).T
        for at in range(0, books, LANES):
            known = (((lane + at) // share) ^ where_ref[0]) * share + (lane + at) % share
            onehot_ref[part, at : at + LANES] = jnp.where(book == known, 1.0, 0.0).astype(BF16)
    for copy, part in zip(own_copies, parts):
        copy.wait()
        first_ref[:, part] = dot(shocks_ref[...], own[:, part])
    for copy in rest_copies:
        copy.wait()


def stage(where, shocks, book_of, loadings, slots, near, far, books):
    rows, depth = shocks.shape
    cols = loadings.shape[1]
    vmem = pl.BlockSpec(memory_space=pltpu.VMEM)
    return pl.pallas_call(
        functools.partial(stage_kernel, slots, near, far),
        out_shape=[
            jax.ShapeDtypeStruct((rows, cols), F32),
            jax.ShapeDtypeStruct((len(near) * depth, cols), BF16),
            jax.ShapeDtypeStruct((len(far) * depth, cols), BF16),
            jax.ShapeDtypeStruct((cols, books), BF16),
        ],
        in_specs=[pl.BlockSpec(memory_space=pltpu.SMEM), vmem, vmem, pl.BlockSpec(memory_space=pltpu.HBM)],
        out_specs=[vmem] * 4,
        scratch_shapes=[pltpu.VMEM((depth, cols), BF16), pltpu.SemaphoreType.DMA((3 + slots,))],
        compiler_params=params(16),
        cost_estimate=pl.CostEstimate(
            flops=2 * rows * depth * cols, bytes_accessed=2 * loadings.size, transcendentals=0
        ),
        name="stage",
    )(where, shocks, book_of, loadings)


def add_moves_kernel(*refs):
    shock_refs, (rest_ref, before_ref, after_ref) = refs[:-3], refs[-3:]
    depth = shock_refs[0].shape[1]
    cols = after_ref.shape[1]
    for part in tiles(cols, cols // 8):
        total = before_ref[:, part]
        for k, shock_ref in enumerate(shock_refs):
            total = total + dot(shock_ref[...], rest_ref[k * depth : (k + 1) * depth, part])
        after_ref[:, part] = total


def add_moves(shocks, rest, before):
    vmem = pl.BlockSpec(memory_space=pltpu.VMEM)
    rows, cols = before.shape
    depth = shocks[0].shape[1]
    return pl.pallas_call(
        add_moves_kernel,
        out_shape=jax.ShapeDtypeStruct((rows, cols), F32),
        in_specs=[vmem] * (len(shocks) + 2),
        out_specs=vmem,
        input_output_aliases={len(shocks) + 1: 0},
        compiler_params=params(16),
        cost_estimate=pl.CostEstimate(
            flops=2 * rows * depth * cols * len(shocks), bytes_accessed=8 * rows * cols, transcendentals=0
        ),
        name="add_moves",
    )(*shocks, rest, before)


def profit_kernel(count, where_ref, *refs):
    top_refs, low_refs = refs[:count], refs[count : 2 * count]
    rest_ref, first_ref, delta_ref, gamma_ref, kappa_ref, onehot_ref = refs[2 * count : 2 * count + 6]
    mine_ref, theirs_ref = refs[2 * count + 6 : 2 * count + 8]
    sum_refs, (total, held, joined, sems) = refs[2 * count + 8 : -4], refs[-4:]
    upper, depth = top_refs[0].shape
    part_cols = mine_ref.shape[1]
    tile = part_cols // 4
    share = sum_refs[0].shape[0]
    for k in range(count):
        joined[k, :upper, :] = top_refs[k][...]
        joined[k, upper:, :] = low_refs[k][...]
    fresh, copies = True, []
    for side, out_ref in ((1 - where_ref[1], held), (where_ref[1], mine_ref)):
        for spot in tiles(part_cols, tile):
            part = pl.ds(pl.multiple_of(side * part_cols + spot.start, tile), tile)
            pieces = []
            for run in tiles(joined.shape[1], ROW_RUN):
                moves = first_ref[run, part]
                for k in range(count):
                    moves = moves + dot(joined[k, run, :], rest_ref[k * depth : (k + 1) * depth, part])
                value = moves * (delta_ref[:, part] + moves * (gamma_ref[:, part] + moves * kappa_ref[:, part]))
                pieces.append(value.astype(BF16))
            profit = jnp.concatenate(pieces, axis=0)
            out_ref[:, spot] = profit
            if out_ref is held:
                copies.append(pltpu.make_async_copy(held.at[:, spot], theirs_ref.at[:, spot], sems.at[len(copies)]))
                copies[-1].start()
            sums = dot(profit, onehot_ref[part, :])
            total[...] = sums if fresh else total[...] + sums
            fresh = False
    turned = total[...].T
    for slot, sum_ref in enumerate(sum_refs):
        sum_ref[...] = turned[slot * share : (slot + 1) * share, :]
    for copy in copies:
        copy.wait()


def profits(where, tops, lows, rest, first, delta, gamma, kappa, onehot, slots):
    rows, cols = first.shape
    books = onehot.shape[1]
    depth = tops[0].shape[1]
    vmem = pl.BlockSpec(memory_space=pltpu.VMEM)
    out_shape = [jax.ShapeDtypeStruct((rows, cols // CORES), BF16)] * 2
    out_shape += [jax.ShapeDtypeStruct((books // slots, rows), F32)] * slots
    return pl.pallas_call(
        functools.partial(profit_kernel, len(tops)),
        out_shape=out_shape,
        in_specs=[pl.BlockSpec(memory_space=pltpu.SMEM)] + [vmem] * (2 * len(tops) + 6),
        out_specs=[vmem, pl.BlockSpec(memory_space=pltpu.HBM)] + [vmem] * slots,
        scratch_shapes=[
            pltpu.VMEM((rows, books), F32),
            pltpu.VMEM((rows, cols // CORES), BF16),
            pltpu.VMEM((len(tops), rows, depth), BF16),
            pltpu.SemaphoreType.DMA((4,)),
        ],
        compiler_params=params(16),
        cost_estimate=pl.CostEstimate(
            flops=2 * rows * cols * (depth * len(tops) + books),
            bytes_accessed=6 * rows * cols,
            transcendentals=0,
        ),
        name="profits",
    )(where, *tops, *lows, rest, first, delta, gamma, kappa, onehot)


def gather_and_revalue(where, shocks, loadings, delta, gamma, kappa, book_of, books):
    slots = lax.axis_size("inst")
    inner = 1
    while inner * inner * 4 <= slots:
        inner *= 2
    outer = slots // inner
    upper = shocks.shape[0] // 16 * UPPER
    along = [f for f in range(1, inner)]
    across = [f * inner for f in range(1, outer)]
    corners = [(a, b) for a in along for b in across]
    near = {f: swap(shocks, "inst", f) for f in along + across}
    first, near_loads, far_loads, onehot = stage(
        where, shocks, book_of, loadings, slots, along + across, [a ^ b for a, b in corners], books
    )
    tops = [swap(near[a][:upper], "inst", b) for a, b in corners]
    lows = [swap(near[b][upper:], "inst", a) for a, b in corners]
    first = add_moves([near[f] for f in along + across], near_loads, first)
    return profits(where, tops, lows, far_loads, first, delta, gamma, kappa, onehot, slots)


def sorting_pairs(n):
    pairs, p = [], 1
    while p < n:
        k = p
        while k:
            for j in range(k % p, n - k, 2 * k):
                for i in range(j, j + min(k, n - j - k)):
                    if i // (2 * p) == (i + k) // (2 * p):
                        pairs.append((i, i + k))
            k //= 2
        p *= 2
    return pairs


def compare(values, pairs):
    for i, j in pairs:
        values[i], values[j] = jnp.minimum(values[i], values[j]), jnp.maximum(values[i], values[j])
    return values


def merged(one, other, most):
    n = len(one)
    if 2 * n <= most:
        values = one + other[::-1]
    else:
        values = [jnp.minimum(a, b) for a, b in zip(one, other[::-1])]
    n = len(values)
    stride = n // 2
    while stride:
        compare(values, [(i, i + stride) for i in range(n) if not i & stride])
        stride //= 2
    return values


def lowest(values, share, most):
    values = compare(list(values), sorting_pairs(len(values)))
    for axis, shift in [(0, 4), (0, 2), (0, 1)] + [(1, shift) for shift in doubling(share, LANES)]:
        values = merged(values, [pltpu.roll(v, shift, axis) for v in values], most)
    return values


def doubling(start, stop):
    while start < stop:
        yield start
        start *= 2


def blocks_of(ref):
    return [ref[at : at + 8, :] for at in range(0, ref.shape[0], 8)]


def book_value_kernel(scale, most, *refs):
    part_refs, (value_ref, list_ref) = refs[:-2], refs[-2:]
    value = part_refs[0][...]
    for part_ref in part_refs[1:]:
        value = value + part_ref[...]
    value = value * scale
    value_ref[...] = value
    share, rows = value.shape
    groups = LANES // share
    depth = rows // groups
    columns = jnp.concatenate([value[:, at : at + depth] for at in range(0, rows, depth)], axis=0).T
    values = lowest([columns[at : at + 8, :] for at in range(0, depth, 8)], share, most)
    place = lax.broadcasted_iota(jnp.int32, (8, LANES), 0)
    place = place + lax.broadcasted_iota(jnp.int32, (8, LANES), 1) // share * 8
    for at in range(0, most, 8 * groups):
        block = values[at]
        for k in range(1, 8 * groups):
            block = jnp.where(place == k, values[at + k], block)
        list_ref[at // groups : at // groups + 8, :] = block


def book_values(scale, most, parts):
    share, rows = parts[0].shape
    return pl.pallas_call(
        functools.partial(book_value_kernel, scale, most),
        out_shape=[
            jax.ShapeDtypeStruct((share, rows), F32),
            jax.ShapeDtypeStruct((most * share // LANES, LANES), F32),
        ],
        compiler_params=params(16),
        name="book_values",
    )(*parts)


def quantile_kernel(most, low_ref, high_ref, rank_ref, value_ref, *refs):
    list_refs, (weight_ref, quantile_ref) = refs[:-2], refs[-2:]
    share, rows = value_ref.shape
    values = lowest([block for ref in list_refs for block in blocks_of(ref)], share, most)
    rank = jnp.broadcast_to(rank_ref[...], (8, LANES))
    sought = values[0]
    for k in range(1, most):
        sought = jnp.where(rank > k, values[k], sought)
    sought = sought[:1, :]
    lower = low_ref[...].astype(F32) * bracket_unit
    upper = high_ref[...].astype(F32) * bracket_unit
    levels = lax.broadcasted_iota(jnp.int32, (PIVOTS, LANES), 0).astype(F32)
    for _ in range(ROUNDS):
        spacing = (upper - lower) / (PIVOTS - 1)
        below = jnp.where(lower + levels * spacing < sought, 1.0, 0.0)
        chosen = jnp.clip(jnp.sum(below, axis=0, keepdims=True), 1.0, float(PIVOTS - 1))
        lower, upper = lower + (chosen - 1.0) * spacing, lower + chosen * spacing
    quantile = (lower + upper) * 0.5
    quantile_ref[...] = jnp.broadcast_to(quantile, quantile_ref.shape)
    column = jnp.broadcast_to(quantile, (LANES, LANES)).T[:share, :]
    column = jnp.concatenate([column] * (rows // LANES), axis=1)
    weight_ref[...] = jax.nn.sigmoid((column - value_ref[...]) / tail_width).astype(BF16)


def quantiles(most, low, high, rank, value, lists):
    share, rows = value.shape
    return pl.pallas_call(
        functools.partial(quantile_kernel, most),
        out_shape=[
            jax.ShapeDtypeStruct((share, rows), BF16),
            jax.ShapeDtypeStruct((8, LANES), F32),
        ],
        compiler_params=params(16),
        name="quantiles",
    )(low, high, rank, value, *lists)


def encode(total, mass):
    top = jnp.maximum(jnp.max(jnp.abs(total), axis=1, keepdims=True), 1e-30)
    level = jnp.ceil(jnp.log(top * (1.0 / top16)) * (finest / octave))
    words = jnp.round(total * jnp.exp(level * (-octave / finest)))
    mass = jnp.maximum(mass, 1e-30)
    power = jnp.ceil(jnp.log(mass) * (1.0 / octave))
    scaled = mass * jnp.exp(power * -octave) * half_word
    upper = jnp.floor(scaled)
    lower = jnp.round((scaled - upper) * half_word)
    column = lax.broadcasted_iota(jnp.int32, (total.shape[0], LANES), 1)
    side = jnp.where(column == 0, level, 0.0)
    side = jnp.where(column == 1, power, side)
    side = jnp.where(column == 2, upper, side)
    side = jnp.where(column == 3, lower, side)
    return words.astype(jnp.int32).astype(jnp.int16), side.astype(jnp.int32).astype(jnp.int16)


def put_words(ref, total, mass):
    words, side = encode(total, mass)
    cols = total.shape[1]
    ref[:, :cols] = words
    ref[:, cols:] = side


def get_words(ref):
    cols = ref.shape[1] - LANES
    side = ref[:, cols:].astype(F32)
    level, power, upper, lower = (side[:, k : k + 1] for k in range(4))
    mass = (upper + lower * (1.0 / half_word)) * (1.0 / half_word) * jnp.exp(power * octave)
    total = ref[:, :cols].astype(F32) * jnp.exp(level * (octave / finest))
    return total, mass


def get_plain(ref):
    cols = ref.shape[1] - LANES
    return ref[:, :cols], ref[:, cols : cols + 1]


def sum_rows(weights, profit_refs, total, spot):
    cols = total.shape[1] - LANES
    for part in tiles(cols, cols // 4):
        result = dot(weights[0], profit_refs[0][:, part])
        for weight, profit_ref in zip(weights[1:], profit_refs[1:]):
            result = result + dot(weight, profit_ref[:, part])
        total[spot, part] = result
    put_mass(weights, total, spot)


def put_mass(weights, total, spot):
    mass = sum(jnp.sum(weight.astype(F32), axis=1, keepdims=True) for weight in weights)
    total[spot, total.shape[1] - LANES :] = jnp.broadcast_to(mass, (mass.shape[0], LANES))


def halves(where_ref, total, line, block):
    half = block // CORES
    for side in range(CORES):
        core = where_ref[1] if side == 0 else 1 - where_ref[1]
        value = total[pl.ds(pl.multiple_of(line * block + core * half, half), half), :]
        yield side, value


def arrange(slots, lines, where_ref, weight_refs, held):
    share = weight_refs[0].shape[0]
    block = share * slots // lines
    piece = min(share, block)
    away = [line for line in range(2, lines, 2)]
    order = away + [1] + [line for line in range(3, lines, 2)] + [0]
    for slot, ref in enumerate(weight_refs):
        for at in range(0, share, piece):
            start = (where_ref[0] ^ slot) * share + at
            line = start // block
            flip = where_ref[2] ^ line
            place = 0
            for k, known in enumerate(order):
                place = place + jnp.where(flip == known, k, 0)
            to = pl.multiple_of(place * block + (start - line * block), piece)
            held[pl.ds(to, piece), :] = ref[at : at + piece, :]
    return len(away) * block


def own_kernel(slots, lines, where_ref, *refs):
    weight_refs, (profit_ref, held, part_ref) = refs[:slots], refs[slots:]
    depth = arrange(slots, lines, where_ref, weight_refs, held)
    sum_rows([held[:depth, :]], [profit_ref], part_ref, slice(0, depth))


def away_kernel(slots, lines, where_ref, *refs):
    weight_refs, (part_ref, profit_ref) = refs[:slots], refs[slots : slots + 2]
    away_refs, (held, total) = refs[slots + 2 : -2], refs[-2:]
    depth = arrange(slots, lines, where_ref, weight_refs, held)
    sum_rows([held[:depth, :]], [profit_ref], total, slice(0, depth))
    total[...] += part_ref[...]
    cols = total.shape[1] - LANES
    block = held.shape[0] // lines
    half = block // CORES
    for k in range(depth // block):
        for side, value in halves(where_ref, total, k, block):
            put_words(away_refs[side].at[k * half : (k + 1) * half, :], value[:, :cols], value[:, cols : cols + 1])


def home_kernel(lines, where_ref, *refs):
    helds, profit_refs = refs[:CORES], refs[CORES : 2 * CORES]
    partner_refs, handled_refs, own_refs = (refs[k : k + 2] for k in range(2 * CORES, 2 * CORES + 6, 2))
    total = refs[-1]
    block = helds[0].shape[0] // lines
    half = block // CORES
    cols = total.shape[1] - LANES
    skip = lines // 2 - 1
    spot = slice(skip * block, lines * block)
    sum_rows([held[spot, :] for held in helds], profit_refs, total, spot)
    for side, value in halves(where_ref, total, skip, block):
        put_words(partner_refs[side], value[:, :cols], value[:, cols : cols + 1])
    for k in range(skip):
        for side, value in halves(where_ref, total, skip + 1 + k, block):
            handled_refs[side][k * half : (k + 1) * half, :] = value
    for side, value in halves(where_ref, total, lines - 1, block):
        own_refs[side][...] = value


def bring_kernel(far_ref, near_ref, sems):
    rows = far_ref.shape[0]
    copies = [
        pltpu.make_async_copy(far_ref.at[run, :], near_ref.at[run, :], sems.at[k])
        for k, run in enumerate(tiles(rows, rows // 8))
    ]
    for copy in copies:
        copy.start()
    for copy in copies:
        copy.wait()


def bring(far):
    return pl.pallas_call(
        bring_kernel,
        out_shape=jax.ShapeDtypeStruct(far.shape, far.dtype),
        in_specs=[pl.BlockSpec(memory_space=pltpu.HBM)],
        out_specs=pl.BlockSpec(memory_space=pltpu.VMEM),
        scratch_shapes=[pltpu.SemaphoreType.DMA((8,))],
        compiler_params=params(16),
        cost_estimate=pl.CostEstimate(flops=0, bytes_accessed=8 * far.size, transcendentals=0),
        name="bring",
    )(far)


def tail_call(kernel, name, out_shape, scratch, where, inputs):
    vmem = pl.BlockSpec(memory_space=pltpu.VMEM)
    return pl.pallas_call(
        kernel,
        out_shape=[jax.ShapeDtypeStruct(shape, kind) for shape, kind in out_shape],
        in_specs=[pl.BlockSpec(memory_space=pltpu.SMEM)] + [vmem] * len(inputs),
        out_specs=[vmem] * len(out_shape),
        scratch_shapes=scratch,
        compiler_params=params(24),
        cost_estimate=pl.CostEstimate(
            flops=0, bytes_accessed=4 * sum(v.size * v.dtype.itemsize for v in inputs), transcendentals=0
        ),
        name=name,
    )(where, *inputs)


def tail_sums(where, weights, others, profit_pair, slots, lines):
    share, rows = weights[0].shape
    cols = profit_pair[0].shape[1]
    books = share * slots
    half = books // lines // CORES
    away_rows = (lines // 2 - 1) * half
    wide = cols + LANES
    held = ((books, rows), BF16)
    part_shape = (away_rows * CORES, wide)
    first, part = tail_call(
        functools.partial(own_kernel, slots, lines),
        "own_sums",
        [held, (part_shape, F32)],
        [],
        where,
        [*weights, profit_pair[0]],
    )
    *away, second = tail_call(
        functools.partial(away_kernel, slots, lines),
        "away_sums",
        [((away_rows, wide), jnp.int16)] * CORES + [held],
        [pltpu.VMEM(part_shape, F32)],
        where,
        [*others, part, profit_pair[1]],
    )
    kinds = [(half, jnp.int16), (away_rows, F32), (half, F32)]
    outs = tail_call(
        functools.partial(home_kernel, lines),
        "home_sums",
        [((n, wide), kind) for n, kind in kinds for _ in range(CORES)],
        [pltpu.VMEM((books, wide), F32)],
        where,
        [first, second, *profit_pair],
    )
    return away, outs[0:2], outs[2:4], outs[4:6]


def relay_kernel(words_ref, plain_ref, out_ref):
    total, mass = get_words(words_ref)
    own_total, own_mass = get_plain(plain_ref)
    put_words(out_ref, total + own_total, mass + own_mass)


def relay(words, plain):
    return pl.pallas_call(
        relay_kernel,
        out_shape=jax.ShapeDtypeStruct(words.shape, jnp.int16),
        compiler_params=params(16),
        name="relay",
    )(words, plain)


def finish_kernel(where_ref, *refs):
    groups, out_ref = (refs[: len(refs) // 2], refs[len(refs) // 2 : -1]), refs[-1]
    cols = groups[0][0].shape[1] - LANES
    for side, group in enumerate(groups):
        total, mass = get_plain(group[0])
        for words_ref in group[1:]:
            more, more_mass = get_words(words_ref)
            total, mass = total + more, mass + more_mass
        core = where_ref[1] if side == 0 else 1 - where_ref[1]
        out_ref[:, pl.ds(pl.multiple_of(core * cols, cols), cols)] = total * (1.0 / mass)


def finish(where, groups):
    half, wide = groups[0][0].shape
    inputs = [*groups[0], *groups[1]]
    vmem = pl.BlockSpec(memory_space=pltpu.VMEM)
    return pl.pallas_call(
        finish_kernel,
        out_shape=jax.ShapeDtypeStruct((half, (wide - LANES) * CORES), F32),
        in_specs=[pl.BlockSpec(memory_space=pltpu.SMEM)] + [vmem] * len(inputs),
        out_specs=vmem,
        compiler_params=params(16),
        name="finish",
    )(where, *inputs)


def body(shocks, loadings, delta, gamma, kappa, book_of, bracket_low, bracket_high, rank):
    inst_cols = loadings.shape[1]
    books = bracket_low.shape[0]
    slots = lax.axis_size("inst")
    lines = lax.axis_size("scen") // CORES
    share = books // slots
    scale = (books / (inst_cols * slots)) ** 0.5
    inst = lax.axis_index("inst")
    scen = lax.axis_index("scen")
    core, line = scen % CORES, scen // CORES
    where = jnp.stack([inst, core, line]).astype(jnp.int32)

    mine, theirs, *sums = gather_and_revalue(
        where,
        shocks,
        loadings,
        delta[None, :],
        gamma[None, :],
        kappa[None, :],
        book_of[None, :],
        books,
    )

    most = shocks.shape[0] * lax.axis_size("scen") // RANK_PART
    own = lambda v: jnp.tile(lax.dynamic_slice_in_dim(v, inst * share, share, 0), LANES // share)[None, :]
    low, high, own_rank = own(bracket_low), own(bracket_high), own(rank)
    parts = [sums[0]] + [swap(sums[slot], "inst", slot) for slot in range(slots - 1, 0, -1)]
    value, lows = book_values(scale, most, parts)
    lows, theirs = lax.optimization_barrier((lows, theirs))
    got = swap(theirs, "scen", 1)
    lists = [lows] + [swap(lows, "scen", CORES * k) for k in [*range(1, lines, 2), *range(2, lines, 2)]]
    lists = lists + [swap(v, "scen", 1) for v in lists]
    weight, row = quantiles(most, low, high, own_rank, value, lists)
    far = {slot: swap(weight, "inst", slot) for slot in range(slots - 1, 0, -1)}
    far[slots - 1], here = lax.optimization_barrier((far[slots - 1], bring(got)))
    weights = [weight] + [far[slot] for slot in range(1, slots)]
    others = [swap(w, "scen", 1) for w in weights]

    away, partner, handled, plain = tail_sums(where, weights, others, [mine, here], slots, lines)
    half = books // lines // CORES
    groups = []
    for side in range(CORES):
        passed = swap(away[side], "scen", CORES)
        sent = relay(passed, handled[side])
        words = []
        for k in range(1, lines // 2):
            block = sent[(k - 1) * half : k * half]
            words.append(swap(block, "scen", (CORES * (2 * k + 1)) ^ side))
        first = plain[0] if side == 0 else swap(plain[1], "scen", 1)
        groups.append([first, swap(partner[side], "scen", CORES ^ side), *words])
    return finish(where, groups), row[0, :share]


def solution(mesh):
    placed = (
        P("scen", "inst"),
        P(None, "inst"),
        P("inst"),
        P("inst"),
        P("inst"),
        P("inst"),
        P(),
        P(),
        P(),
    )
    return jax.shard_map(
        body, mesh=mesh, in_specs=placed, out_specs=(P("scen", "inst"), P("inst")), check_vma=False
    )
```
